256 devices in a mesh: cam: 4 (over y), dev: 64 (over x, z, core).
Axes of the slice: x: 4, y: 4, z: 8, core: 2. Of those that a mesh axis runs over, the one named last changes fastest.
Arguments:
- params: float32 [2048, 59, 128], P('dev'), may hold values from -4 to 4
- moment_first: float32 [64, 4, 8, 59, 128], P('dev', 'cam'), may hold values from -3 to 3
- moment_second: float32 [64, 4, 8, 59, 128], P('dev', 'cam'), may hold values from 0.01 to 1
- cam_proj: float32 [8, 9, 59], P('cam'), may hold values from -0.75 to 0.75
- send_block: int32 [8, 64, 64, 1], P('cam', 'dev'), may hold values from 0 to 31
- tile_slot: int32 [8, 128, 8], P('cam', 'dev'), may hold values from 0 to 63, as said below
- tile_count: int32 [8, 128], P('cam', 'dev'), may hold values from 2 to 8, as said below
- targets: float32 [8, 128, 3, 256], P('cam', 'dev'), may hold values from 0 to 1
- split_block: int32 [64, 64], P('dev'), may hold values from 0 to 31, as said below
- split_live: int32 [64, 64], P('dev'), may hold values from 0 to 1, as said below
Outputs:
- images: float32 [8, 128, 3, 256], P('cam', 'dev')
- new_params: float32 [2048, 59, 128], P('dev')
- new_first: float32 [64, 4, 8, 59, 128], P('dev', 'cam')
- new_second: float32 [64, 4, 8, 59, 128], P('dev', 'cam')
- children: float32 [4096, 2, 59, 128], P('dev')
The draws below stay inside these ranges and needn't reach their ends.
Inputs may be any that keep to these rules, and one draw needn't show every extreme that they name: `tile_count`: in every camera some tile has exactly 8 live entries. `tile_slot`: the entries of one tile's list are distinct; entries at positions from the tile's count on are not read. `split_block`: among an owner's entries where split_live is 1 the blocks are distinct. `split_live`: each row holds exactly 16 ones; in every draw some new owner has a one in every row.
All inputs are finite; a program needn't handle non-finite values.
Results may differ from the reference program's by a relative error of at most 0.0003.
Values sent between devices are 32-bit elements; how exact they have to be, the bound alone decides.
No kernel may reach another device: no remote copies, remote signals or barrier semaphores. Data moves between devices by JAX's collectives and lax.ppermute only.
A program may use at most 64 MiB of HBM per device.

```python
import math
import jax
import jax.numpy as jnp
from jax import lax

F = 59
SPL = 128
TSIDE = 16
PIX = 256
PROJ = 9
KMAX = 8
BLK_DEV = 32
TILE_DEV = 2
OWNERS = 64
GROUPS = 4
CAMERAS = 8
TILES = 128
NBLK = 2048
BQ = 8
CAP = 1
SLOTS = 64
SPLIT_DEV = 16


def depth_lists(key):
    folded = jax.random.fold_in(key, 7101)
    key_level, key_heavy, key_count, key_order = jax.random.split(folded, 4)
    load_level = jax.random.randint(key_level, (CAMERAS, OWNERS), max(1, KMAX // 2), KMAX + 1)
    heavy_owner = jax.random.randint(key_heavy, (CAMERAS, 1), 0, OWNERS)
    owner_ids = jnp.arange(OWNERS, dtype=jnp.int32)[None, :]
    load_level = jnp.where(owner_ids == heavy_owner, KMAX, load_level)
    lowest = jnp.maximum(load_level // 2, 1)
    tile_counts = jax.random.randint(key_count, (CAMERAS, OWNERS, TILE_DEV), lowest[:, :, None], load_level[:, :, None] + 1)
    first_tile = jnp.arange(TILE_DEV, dtype=jnp.int32)[None, None, :] == 0
    tile_counts = jnp.where((owner_ids[:, :, None] == heavy_owner[:, :, None]) & first_tile, KMAX, tile_counts)
    tile_counts = tile_counts.reshape(CAMERAS, TILES).astype(jnp.int32)
    scores = jax.random.randint(key_order, (CAMERAS, TILES, SLOTS), 0, 1 << 20) * SLOTS + jnp.arange(SLOTS, dtype=jnp.int32)
    slot_order = jnp.argsort(scores, axis=-1)[:, :, :KMAX].astype(jnp.int32)
    return (slot_order, tile_counts)


def draw_tile_slot(key, part):
    return depth_lists(key)[0]


def draw_tile_count(key, part):
    return depth_lists(key)[1]


def split_plan(key):
    folded = jax.random.fold_in(key, 7202)
    key_popular, key_target, key_rank, key_block = jax.random.split(folded, 4)
    popular = jax.random.randint(key_popular, (OWNERS,), 0, 4)
    favoured = jax.random.randint(key_target, (), 0, OWNERS)
    owner_ids = jnp.arange(OWNERS, dtype=jnp.int32)
    popular = jnp.where(owner_ids == favoured, 4, popular)
    scores = (popular[None, :] * (1 << 16) + jax.random.randint(key_rank, (OWNERS, OWNERS), 0, 1 << 16)) * OWNERS + owner_ids[None, :]
    dest_rank = jnp.argsort(jnp.argsort(-scores, axis=1), axis=1).astype(jnp.int32)
    live_mask = (dest_rank < SPLIT_DEV).astype(jnp.int32)
    block_scores = jax.random.randint(key_block, (OWNERS, BLK_DEV), 0, 1 << 20) * BLK_DEV + jnp.arange(BLK_DEV, dtype=jnp.int32)[None, :]
    blocks = jnp.argsort(block_scores, axis=1).astype(jnp.int32)
    chosen = jnp.take_along_axis(blocks, dest_rank % BLK_DEV, axis=1)
    return (chosen.astype(jnp.int32), live_mask)


def draw_split_block(key, part):
    return split_plan(key)[0]


def draw_split_live(key, part):
    return split_plan(key)[1]


def set_ends(array, own_key, low, high):
    shape = array.shape
    index_at = [jax.random.randint(jax.random.fold_in(own_key, axis), (), 0, shape[axis]) for axis in range(len(shape))]
    array = array.at[tuple(index_at)].set(low)
    longest = shape.index(max(shape))
    index_at[longest] = (index_at[longest] + 1) % shape[longest]
    return array.at[tuple(index_at)].set(high)


def steps_of(rng, extent, shards, smallest, high):
    gain, own = 1.0, jax.random.fold_in(rng, 6)
    for position, blocks in shards:
        heights = jnp.exp(jax.random.uniform(jax.random.fold_in(own, position), (blocks,), jnp.float32, smallest / len(shards), high / len(shards)))
        gain = gain * jnp.repeat(heights, extent[position] // blocks).reshape([-1 if axis == position else 1 for axis in range(len(extent))])
    return gain


def centred(rng, dims, deviation, reach, cuts=(), kind=jnp.bfloat16):
    result = deviation * jax.random.normal(rng, dims, jnp.float32)
    if cuts:
        result = result * steps_of(rng, dims, cuts, -0.22, 0.18)
    return jnp.clip(result, -reach, reach).astype(kind)


def setup_inputs(seed: int = 0) -> dict:
    streams_of = jax.random.split(jax.random.key(seed), 11)
    params = centred(streams_of[0], (NBLK, F, SPL), 1.0, 4.0, ((0, 64),), jnp.float32)
    moment_first = centred(streams_of[1], (OWNERS, GROUPS, BQ, F, SPL), 0.5, 3.0, ((0, 64), (1, 4)), jnp.float32)
    moment_second = jnp.clip(jnp.exp(math.log(1.0) - 4.6051702 * jax.random.uniform(streams_of[2], (OWNERS, GROUPS, BQ, F, SPL), jnp.float32) ** steps_of(streams_of[2], (OWNERS, GROUPS, BQ, F, SPL), ((0, 64), (1, 4)), -0.2, 0.2)), 0.01, 1.0)
    cam_proj = centred(streams_of[3], (CAMERAS, PROJ, F), F ** -0.5, 0.75, ((0, 4),), jnp.float32)
    send_block = set_ends(jax.random.randint(streams_of[4], (CAMERAS, OWNERS, OWNERS, CAP), 0, BLK_DEV), jax.random.fold_in(streams_of[4], 1), 0, BLK_DEV - 1).astype(jnp.int32)
    tile_slot = draw_tile_slot(jax.random.fold_in(streams_of[10], 71), 0)
    tile_count = draw_tile_count(jax.random.fold_in(streams_of[10], 71), 0)
    targets = jnp.clip(1.0 * jax.random.uniform(streams_of[7], (CAMERAS, TILES, 3, PIX), jnp.float32) ** steps_of(streams_of[7], (CAMERAS, TILES, 3, PIX), ((0, 4), (1, 64)), -0.2, 0.2), 0.0, 1.0)
    split_block = draw_split_block(jax.random.fold_in(streams_of[10], 71), 0)
    split_live = draw_split_live(jax.random.fold_in(streams_of[10], 71), 0)
    return {"params": params, "moment_first": moment_first, "moment_second": moment_second, "cam_proj": cam_proj, "send_block": send_block, "tile_slot": tile_slot, "tile_count": tile_count, "targets": targets, "split_block": split_block, "split_live": split_live}


LOSS_WEIGHT = 256.0
RATE = 0.01
BETA_FIRST = 0.9
BETA_SECOND = 0.999
EPSILON = 1e-08
SHRINK = math.log(1.6)
PRECISE = lax.Precision.HIGHEST

def unpack(projected):
    centre = 0.5 * TSIDE
    spread = 0.375 * TSIDE
    mean_x = centre + spread * jnp.tanh(projected[:, 0])
    mean_y = centre + spread * jnp.tanh(projected[:, 1])
    conic_a = 0.02 + 0.1 * jax.nn.softplus(projected[:, 2])
    conic_c = 0.02 + 0.1 * jax.nn.softplus(projected[:, 4])
    conic_b = 0.9 * jnp.sqrt(conic_a * conic_c) * jnp.tanh(projected[:, 3])
    opacity = 0.99 * jax.nn.sigmoid(projected[:, 5] - 6.0)
    shape_part = jnp.stack([mean_x, mean_y, conic_a, conic_b, conic_c, opacity], axis=1)
    return jnp.concatenate([shape_part, jax.nn.sigmoid(projected[:, 6:9])], axis=1)

def project(params, matrix):
    projected = jnp.einsum('pf,bfs->bps', matrix, params, precision=PRECISE)
    return unpack(projected)

def footprint(features, active, grid_x, grid_y):
    off_x = grid_x[None, None, :] - features[:, 0, :, None]
    off_y = grid_y[None, None, :] - features[:, 1, :, None]
    exponent = 0.5 * (features[:, 2, :, None] * off_x * off_x + 2.0 * features[:, 3, :, None] * off_x * off_y + features[:, 4, :, None] * off_y * off_y)
    falloff = jnp.exp(-exponent) * active[:, None, None]
    alpha_term = features[:, 5, :, None] * falloff
    return (off_x, off_y, falloff, alpha_term)

def divide(parents):
    offset = 0.5 * jnp.exp(parents[:, 3:6] - 1.0)
    shrunk = parents[:, 3:6] - SHRINK
    remainder = parents[:, 6:]
    child_plus = jnp.concatenate([parents[:, 0:3] + offset, shrunk, remainder], axis=1)
    child_minus = jnp.concatenate([parents[:, 0:3] - offset, shrunk, remainder], axis=1)
    return jnp.stack([child_plus, child_minus], axis=1)

def reference(params, moment_first, moment_second, cam_proj, send_block, tile_slot, tile_count, targets, split_block, split_live):
    pixel_ids = jnp.arange(TSIDE * TSIDE, dtype=jnp.int32)
    grid_x = (pixel_ids % TSIDE).astype(jnp.float32) + 0.5
    grid_y = (pixel_ids // TSIDE).astype(jnp.float32) + 0.5
    owner_ids = jnp.arange(TILES, dtype=jnp.int32) // TILE_DEV
    source_ids = (tile_slot // CAP).astype(jnp.int32)
    within_ids = (tile_slot % CAP).astype(jnp.int32)
    camera_ids = jnp.arange(CAMERAS, dtype=jnp.int32)[:, None, None]
    block_of = (source_ids * BLK_DEV + send_block[camera_ids, source_ids, owner_ids[None, :, None], within_ids]).astype(jnp.int32)
    live_rows = (jnp.arange(KMAX, dtype=jnp.int32)[None, None, :] < tile_count[:, :, None]).astype(jnp.float32)

    def tile_group(features_all, group_blocks, group_live):

        def advance(state_carry, inputs):
            transmit, colour = state_carry
            blocks_now, live_now = inputs
            features = jnp.take(features_all, blocks_now, axis=0)
            unused_x, unused_y, unused_fall, alpha_term = footprint(features, live_now, grid_x, grid_y)
            log_keep = jnp.log1p(-alpha_term)
            log_before = jnp.cumsum(log_keep, axis=1) - log_keep
            weights = alpha_term * transmit[:, None, :] * jnp.exp(log_before)
            colour = colour + jnp.einsum('dcs,dsp->dcp', features[:, 6:9], weights, precision=PRECISE)
            transmit = transmit * jnp.exp(lax.optimization_barrier(jnp.sum(log_keep, axis=1)))
            return ((transmit, colour), None)
        tile_rows = group_blocks.shape[0]
        start_state = (jnp.ones((tile_rows, PIX), jnp.float32), jnp.zeros((tile_rows, 3, PIX), jnp.float32))
        scanned = lax.scan(jax.checkpoint(advance), start_state, (group_blocks.T, group_live.T))
        return scanned[0][1]

    def loss_all(values):

        def per_camera(inputs):
            matrix, blocks_cam, live_cam, target_cam = inputs
            features_all = project(values, matrix)

            def per_group(group_data):
                return tile_group(features_all, group_data[0], group_data[1])
            grouped = lax.map(jax.checkpoint(per_group), (blocks_cam.reshape(OWNERS, TILE_DEV, KMAX), live_cam.reshape(OWNERS, TILE_DEV, KMAX)))
            colour = grouped.reshape(TILES, 3, PIX)
            error = colour - target_cam
            return (0.5 * LOSS_WEIGHT * jnp.sum(error * error), colour)
        losses, colours = lax.map(jax.checkpoint(per_camera), (cam_proj, block_of, live_rows, targets))
        return (jnp.sum(losses), colours)
    gradient, images = jax.grad(loss_all, has_aux=True)(params)
    first_moment = moment_first.reshape(params.shape)
    second_moment = moment_second.reshape(params.shape)
    new_first = BETA_FIRST * first_moment + (1.0 - BETA_FIRST) * gradient
    new_second = BETA_SECOND * second_moment + (1.0 - BETA_SECOND) * gradient * gradient
    new_params = params - RATE * new_first / (jnp.sqrt(new_second) + EPSILON)
    parent_ids = (jnp.arange(OWNERS, dtype=jnp.int32)[None, :] * BLK_DEV + split_block.T).astype(jnp.int32)
    live_mask = split_live.T.reshape(-1).astype(jnp.float32)
    parents = jnp.take(new_params, parent_ids.reshape(-1), axis=0)
    children = divide(parents) * live_mask[:, None, None, None]
    return (images, new_params, new_first.reshape(moment_first.shape), new_second.reshape(moment_second.shape), children)
```

```python
import functools
import math

import jax
import jax.numpy as jnp
from jax import lax
from jax.experimental import pallas as pl
from jax.experimental.pallas import tpu as pltpu
from jax.sharding import PartitionSpec as P

TSIDE = 16
PIX = TSIDE * TSIDE
LANES = 128
PROJ = 9
FIELDS = 59
QUARTER = 15
PIECE = 16

LOSS_WEIGHT = 256.0
RATE = 0.01
BETA_FIRST = 0.9
BETA_SECOND = 0.999
EPSILON = 1e-08
SHRINK = math.log(1.6)
LOG2E = math.log2(math.e)

VMEM = pl.BlockSpec(memory_space=pltpu.VMEM)
SMEM = pl.BlockSpec(memory_space=pltpu.SMEM)
PARAMS = pltpu.CompilerParams(vmem_limit_bytes=40 * 1024 * 1024)


def softplus(values):
    return jnp.maximum(values, 0.0) + jnp.log1p(jnp.exp(-jnp.abs(values)))


def sigmoid(values):
    return 1.0 / (1.0 + jnp.exp(-values))


def project_kernel(proj_ref, send_ref, params_ref, out_ref, raw_ref, feat_ref):
    centre, spread = 0.5 * TSIDE, 0.375 * TSIDE
    fields = params_ref.shape[0]
    for camera in range(2):
        raw = [None] * PROJ
        for field in range(fields):
            row = params_ref[field]
            for p in range(PROJ):
                term = proj_ref[camera, p, field] * row
                raw[p] = term if field == 0 else raw[p] + term
        for p in range(PROJ):
            raw_ref[camera * PROJ + p] = raw[p]
    for camera in range(2):
        first = camera * PROJ
        raw = [raw_ref[first + p] for p in range(PROJ)]
        conic_a = 0.02 + 0.1 * softplus(raw[2])
        conic_c = 0.02 + 0.1 * softplus(raw[4])
        feat_ref[first + 0] = centre + spread * jnp.tanh(raw[0])
        feat_ref[first + 1] = centre + spread * jnp.tanh(raw[1])
        feat_ref[first + 2] = conic_a
        feat_ref[first + 3] = 0.9 * jnp.sqrt(conic_a * conic_c) * jnp.tanh(raw[3])
        feat_ref[first + 4] = conic_c
        feat_ref[first + 5] = 0.99 * sigmoid(raw[5] - 6.0)
        for p in range(6, PROJ):
            feat_ref[first + p] = sigmoid(raw[p])

    def place(j, unused):
        for camera in range(2):
            block = send_ref[camera, j]
            for p in range(PROJ):
                out_ref[j, p, pl.ds(camera, 1), :] = feat_ref[camera * PROJ + p, pl.ds(block, 1), :]
        return unused

    lax.fori_loop(0, out_ref.shape[0], place, 0, unroll=4)


def render_kernel(
    slot_ref,
    count_ref,
    recv_ref,
    target_ref,
    back_ref,
    image_ref,
    alpha_ref,
    reach_ref,
    acc_ref,
    cot_ref,
    carry_ref,
):
    lane = lax.broadcasted_iota(jnp.int32, (PIX, LANES), 1)
    sub = lax.broadcasted_iota(jnp.int32, (8, LANES), 0).astype(jnp.float32)
    column = [sub + 0.5, sub + 8.5]
    back_ref[...] = jnp.zeros(back_ref.shape, jnp.float32)
    image_ref[...] = jnp.zeros(image_ref.shape, jnp.float32)

    def tile(index, unused):
        camera = index // 2
        which = index % 2
        count = count_ref[camera, which]
        acc_ref[...] = jnp.zeros(acc_ref.shape, jnp.float32)
        carry_ref[...] = jnp.ones(carry_ref.shape, jnp.float32)

        def wide(slot, p):
            return jnp.broadcast_to(recv_ref[slot, p, pl.ds(camera, 1), :], (8, LANES))

        def forward(k, unused):
            slot = slot_ref[camera, which, k]
            off_x = [c - wide(slot, 0) for c in column]
            mean_y = wide(slot, 1)
            half_a = (-0.5 * LOG2E) * wide(slot, 2)
            full_b = -LOG2E * wide(slot, 3)
            half_c = (-0.5 * LOG2E) * wide(slot, 4)
            square_x = [half_a * d * d for d in off_x]
            rows = []
            for y in range(TSIDE):
                off_y = (y + 0.5) - mean_y
                cross = full_b * off_y
                square_y = half_c * off_y * off_y
                for half in range(2):
                    rows.append(square_x[half] + (cross * off_x[half] + square_y))
            alpha = recv_ref[slot, 5, pl.ds(camera, 1), :] * jnp.exp2(jnp.concatenate(rows, axis=0))
            keep = 1.0 - alpha
            reach = jnp.where(lane == 0, carry_ref[...], pltpu.roll(keep, 1, 1))
            shift = 1
            while shift < LANES:
                reach = reach * jnp.where(lane >= shift, pltpu.roll(reach, shift, 1), 1.0)
                shift *= 2
            alpha_ref[k] = alpha
            reach_ref[k] = reach
            weights = alpha * reach
            for c in range(3):
                acc_ref[c] = acc_ref[c] + recv_ref[slot, 6 + c, pl.ds(camera, 1), :] * weights
            carry_ref[...] = jnp.broadcast_to((reach * keep)[:, LANES - 1 :], (PIX, LANES))
            return unused

        lax.fori_loop(0, count, forward, 0)
        for c in range(3):
            colour = jnp.sum(acc_ref[c], axis=1, keepdims=True)
            place = index * 3 + c
            image_ref[...] = jnp.where(lane == place, colour, image_ref[...])
            target = pltpu.roll(target_ref[...], LANES - place, 1)[:, :1]
            cot_ref[c] = jnp.broadcast_to(LOSS_WEIGHT * (colour - target), (PIX, LANES))
        carry_ref[...] = jnp.zeros(carry_ref.shape, jnp.float32)

        def backward(step, unused):
            k = count - 1 - step
            slot = slot_ref[camera, which, k]
            alpha = alpha_ref[k]
            weights = alpha * reach_ref[k]
            shade = recv_ref[slot, 6, pl.ds(camera, 1), :] * cot_ref[0]
            for c in range(1, 3):
                shade = shade + recv_ref[slot, 6 + c, pl.ds(camera, 1), :] * cot_ref[c]
            shade = shade * weights
            behind = jnp.where(lane == LANES - 1, carry_ref[...], pltpu.roll(shade, LANES - 1, 1))
            shift = 1
            while shift < LANES:
                behind = behind + jnp.where(lane < LANES - shift, pltpu.roll(behind, LANES - shift, 1), 0.0)
                shift *= 2
            carry_ref[...] = jnp.broadcast_to((behind + shade)[:, :1], (PIX, LANES))
            pull = shade - behind * alpha / (1.0 - alpha)
            off_x = [c - wide(slot, 0) for c in column]
            mean_y = wide(slot, 1)
            plain, first_y, second_y = [None] * 2, [None] * 2, [None] * 2
            for y in range(TSIDE):
                off_y = (y + 0.5) - mean_y
                for half in range(2):
                    start = (2 * y + half) * 8
                    part = pull[start : start + 8]
                    once = off_y * part
                    twice = off_y * once
                    if y == 0:
                        plain[half], first_y[half], second_y[half] = part, once, twice
                    else:
                        plain[half] = plain[half] + part
                        first_y[half] = first_y[half] + once
                        second_y[half] = second_y[half] + twice

            def total(values):
                return jnp.sum(values, axis=0, keepdims=True)

            along_x = [off_x[half] * plain[half] for half in range(2)]
            sum_0 = total(plain[0] + plain[1])
            sum_x = total(along_x[0] + along_x[1])
            sum_y = total(first_y[0] + first_y[1])
            sum_xx = total(off_x[0] * along_x[0] + off_x[1] * along_x[1])
            sum_xy = total(off_x[0] * first_y[0] + off_x[1] * first_y[1])
            sum_yy = total(second_y[0] + second_y[1])
            conic_a = recv_ref[slot, 2, pl.ds(camera, 1), :]
            conic_b = recv_ref[slot, 3, pl.ds(camera, 1), :]
            conic_c = recv_ref[slot, 4, pl.ds(camera, 1), :]
            grads = [
                conic_a * sum_x + conic_b * sum_y,
                conic_b * sum_x + conic_c * sum_y,
                -0.5 * sum_xx,
                -sum_xy,
                -0.5 * sum_yy,
                sum_0,
            ]
            for c in range(3):
                product = cot_ref[c] * weights
                grads.append(total(jnp.sum(product.reshape(PIX // 8, 8, LANES), axis=0)))
            for p in range(PROJ):
                spot = (slot, p, pl.ds(camera, 1), slice(None))
                back_ref[spot] = back_ref[spot] + grads[p]
            return unused

        lax.fori_loop(0, count, backward, 0)
        return unused

    lax.fori_loop(0, 4, tile, 0)


def collect_kernel(send_ref, back_ref, raw_ref, out_ref, acc_ref):
    acc_ref[...] = jnp.zeros(acc_ref.shape, jnp.float32)

    def gather(j, unused):
        for camera in range(2):
            block = send_ref[camera, j]
            for p in range(PROJ):
                spot = (camera * PROJ + p, pl.ds(block, 1), slice(None))
                acc_ref[spot] = acc_ref[spot] + back_ref[j, p, pl.ds(camera, 1), :]
        return unused

    lax.fori_loop(0, back_ref.shape[0], gather, 0)
    spread = 0.375 * TSIDE
    share = out_ref.shape[2]
    for camera in range(2):
        first = camera * PROJ
        raw = [raw_ref[first + p] for p in range(PROJ)]
        grad = [acc_ref[first + p] for p in range(PROJ)]
        conic_a = 0.02 + 0.1 * softplus(raw[2])
        conic_c = 0.02 + 0.1 * softplus(raw[4])
        root = 0.9 * jnp.sqrt(conic_a * conic_c)
        turn = jnp.tanh(raw[3])
        from_b = 0.5 * grad[3] * root * turn
        tan_x, tan_y = jnp.tanh(raw[0]), jnp.tanh(raw[1])
        result = [
            grad[0] * spread * (1.0 - tan_x * tan_x),
            grad[1] * spread * (1.0 - tan_y * tan_y),
            (grad[2] + from_b / conic_a) * 0.1 * sigmoid(raw[2]),
            grad[3] * root * (1.0 - turn * turn),
            (grad[4] + from_b / conic_c) * 0.1 * sigmoid(raw[4]),
            grad[5] * (1.0 - sigmoid(raw[5] - 6.0)),
        ]
        for p in range(6, PROJ):
            shade = sigmoid(raw[p])
            result.append(grad[p] * shade * (1.0 - shade))
        for p in range(PROJ):
            for group in range(out_ref.shape[0]):
                out_ref[group, first + p] = result[p][group * share : (group + 1) * share]


def adam_kernel(
    place_ref, proj_ref, pull_ref, params_ref, first_ref, second_ref, new_first_ref, new_second_ref, new_ref, piece_ref
):
    groups, rows = pull_ref.shape[0], pull_ref.shape[1]
    share = pull_ref.shape[2]
    start = pl.multiple_of(place_ref[0] * share, share)
    step = 12
    for low in range(0, FIELDS, step):
        fields = range(low, min(low + step, FIELDS))
        grads = [None] * len(fields)
        for group in range(groups):
            for row in range(rows):
                value = pull_ref[group, row]
                for at, field in enumerate(fields):
                    term = proj_ref[group * rows + row, field] * value
                    grads[at] = term if grads[at] is None else grads[at] + term
        for at, field in enumerate(fields):
            grad = grads[at]
            new_first = BETA_FIRST * first_ref[field] + (1.0 - BETA_FIRST) * grad
            new_second = BETA_SECOND * second_ref[field] + (1.0 - BETA_SECOND) * grad * grad
            old = params_ref[field, pl.ds(start, share), :]
            new = old - RATE * new_first / (jnp.sqrt(new_second) + EPSILON)
            new_first_ref[field] = new_first
            new_second_ref[field] = new_second
            new_ref[field] = new
            piece_ref[field // QUARTER, field % QUARTER] = new
            if field == FIELDS - 1:
                for extra in range(FIELDS, 4 * QUARTER):
                    piece_ref[extra // QUARTER, extra % QUARTER] = new


def parents_kernel(block_ref, live_ref, piece_ref, out_ref):
    share = piece_ref.shape[2]

    def place(j, unused):
        block = block_ref[0, j]
        group = block // share
        within = block % share
        for field in range(QUARTER):
            out_ref[j, pl.ds(field, 1), :] = piece_ref[group, field, pl.ds(within, 1), :]
        live = live_ref[0, j].astype(jnp.float32)
        out_ref[j, pl.ds(QUARTER, 1), :] = jnp.full((1, LANES), live, jnp.float32)
        return unused

    lax.fori_loop(0, out_ref.shape[0], place, 0, unroll=4)


def children_kernel(place_ref, own_ref, before_ref, after_ref, far_low_ref, far_high_ref, out_ref):
    step = pl.program_id(0)
    half = pl.num_programs(0) // 2

    def fill(ref, offset):
        quarter = lax.rem(place_ref[0] + offset, 4)
        first = quarter == 0

        def one(j, unused):
            live = ref[j, pl.ds(QUARTER, 1), :] > 0.5
            rows = [ref[j, pl.ds(field, 1), :] for field in range(QUARTER)]
            for field in range(QUARTER):
                at = jnp.minimum(quarter * QUARTER + field, FIELDS - 1)
                if field < 3:
                    off = jnp.where(first, 0.5 * jnp.exp(rows[field + 3] - 1.0), 0.0)
                    out_ref[j, at, pl.ds(0, 1), :] = jnp.where(live, rows[field] + off, 0.0)
                    out_ref[j, at, pl.ds(1, 1), :] = jnp.where(live, rows[field] - off, 0.0)
                else:
                    row = rows[field]
                    if field < 6:
                        row = row - jnp.where(first, SHRINK, 0.0)
                    out_ref[j, at] = jnp.broadcast_to(jnp.where(live, row, 0.0), (2, LANES))
            return unused

        lax.fori_loop(0, out_ref.shape[0], one, 0)

    fill(own_ref, 0)
    fill(before_ref, 3)
    fill(after_ref, 1)

    @pl.when(step < half)
    def _():
        fill(far_low_ref, 2)

    @pl.when(step >= half)
    def _():
        fill(far_high_ref, 2)


def shape(*dims):
    return jax.ShapeDtypeStruct(dims, jnp.float32)


def shift_by(values, distance):
    size = lax.axis_size("cam")
    return lax.ppermute(values, "cam", [(i, (i + distance) % size) for i in range(size)])


def body(
    params,
    moment_first,
    moment_second,
    cam_proj,
    send_block,
    tile_slot,
    tile_count,
    targets,
    split_block,
    split_live,
):
    owned = params.shape[0]
    owners = split_block.shape[1]
    groups = lax.axis_size("cam")
    share = owned // groups
    place = lax.axis_index("cam").astype(jnp.int32).reshape(1)
    by_field = params.transpose(1, 0, 2)
    send = send_block.reshape(2, owners)
    wire = shape(owners, PROJ, 2, LANES)

    with jax.named_scope("project"):
        outgoing, raw = pl.pallas_call(
            project_kernel,
            out_shape=(wire, shape(2 * PROJ, owned, LANES)),
            in_specs=[SMEM, SMEM, VMEM],
            out_specs=(VMEM, VMEM),
            scratch_shapes=[pltpu.VMEM((2 * PROJ, owned, LANES), jnp.float32)],
            compiler_params=PARAMS,
        )(cam_proj, send, by_field)
    received = lax.all_to_all(outgoing, "dev", split_axis=0, concat_axis=0, tiled=True)
    target = jnp.pad(targets.reshape(12, PIX).T, ((0, 0), (0, LANES - 12)))
    with jax.named_scope("render"):
        returning, pictures = pl.pallas_call(
            render_kernel,
            out_shape=(wire, shape(PIX, LANES)),
            in_specs=[SMEM, SMEM, VMEM, VMEM],
            out_specs=(VMEM, VMEM),
            scratch_shapes=[
                pltpu.VMEM((8, PIX, LANES), jnp.float32),
                pltpu.VMEM((8, PIX, LANES), jnp.float32),
                pltpu.VMEM((3, PIX, LANES), jnp.float32),
                pltpu.VMEM((3, PIX, LANES), jnp.float32),
                pltpu.VMEM((PIX, LANES), jnp.float32),
            ],
            compiler_params=PARAMS,
        )(tile_slot, tile_count, received, target)
    images = pictures[:, :12].T.reshape(targets.shape)
    returned = lax.all_to_all(returning, "dev", split_axis=0, concat_axis=0, tiled=True)
    with jax.named_scope("collect"):
        pulls = pl.pallas_call(
            collect_kernel,
            out_shape=shape(groups, 2 * PROJ, share, LANES),
            in_specs=[SMEM, VMEM, VMEM],
            out_specs=VMEM,
            scratch_shapes=[pltpu.VMEM((2 * PROJ, owned, LANES), jnp.float32)],
            compiler_params=PARAMS,
        )(send, returned, raw)
    all_proj = lax.all_gather(cam_proj, "cam", axis=0, tiled=True).reshape(-1, FIELDS)
    pulls = lax.all_to_all(pulls, "cam", split_axis=0, concat_axis=0, tiled=True)

    def moments(values):
        return values.reshape(share, FIELDS, LANES).transpose(1, 0, 2)

    def back(values):
        return values.transpose(1, 0, 2).reshape(moment_first.shape)

    own = shape(FIELDS, share, LANES)
    with jax.named_scope("adam"):
        new_first, new_second, new_share, pieces = pl.pallas_call(
            adam_kernel,
            out_shape=(own, own, own, shape(groups, QUARTER, share, LANES)),
            in_specs=[SMEM, SMEM, VMEM, VMEM, VMEM, VMEM],
            out_specs=(VMEM, VMEM, VMEM, VMEM),
            compiler_params=PARAMS,
        )(place, all_proj, pulls, by_field, moments(moment_first), moments(moment_second))
    pieces = lax.all_to_all(pieces, "cam", split_axis=0, concat_axis=0, tiled=True)
    new_params = lax.all_gather(new_share, "cam", axis=1, tiled=True)
    with jax.named_scope("parents"):
        parents = pl.pallas_call(
            parents_kernel,
            out_shape=shape(owners, PIECE, LANES),
            in_specs=[SMEM, SMEM, VMEM],
            out_specs=VMEM,
            compiler_params=PARAMS,
        )(split_block, split_live, pieces)
    parents = lax.all_to_all(parents, "dev", split_axis=0, concat_axis=0, tiled=True)
    half = owners // 2
    before = shift_by(parents, 1)
    after = shift_by(parents, 3)
    far_low = shift_by(before[:half], 1)
    far_high = shift_by(after[half:], 3)
    rows = 8
    steps = owners // rows

    def block(index):
        return pl.BlockSpec((rows, PIECE, LANES), index)

    with jax.named_scope("children"):
        children = pl.pallas_call(
            children_kernel,
            grid=(steps,),
            out_shape=shape(owners, FIELDS, 2, LANES),
            in_specs=[
                SMEM,
                block(lambda i: (i, 0, 0)),
                block(lambda i: (i, 0, 0)),
                block(lambda i: (i, 0, 0)),
                block(lambda i: (jnp.minimum(i, steps // 2 - 1), 0, 0)),
                block(lambda i: (jnp.maximum(i - steps // 2, 0), 0, 0)),
            ],
            out_specs=pl.BlockSpec((rows, FIELDS, 2, LANES), lambda i: (i, 0, 0, 0)),
            compiler_params=PARAMS,
        )(place, parents, before, after, far_low, far_high)
    return (
        images,
        new_params.transpose(1, 0, 2),
        back(new_first),
        back(new_second),
        children.transpose(0, 2, 1, 3),
    )


def solution(mesh):
    placed = (
        P("dev", None, None),
        P("dev", "cam", None, None, None),
        P("dev", "cam", None, None, None),
        P("cam", None, None),
        P("cam", "dev", None, None),
        P("cam", "dev", None),
        P("cam", "dev"),
        P("cam", "dev", None, None),
        P("dev", None),
        P("dev", None),
    )
    return jax.shard_map(
        body,
        mesh=mesh,
        in_specs=placed,
        out_specs=(
            P("cam", "dev", None, None),
            P("dev", None, None),
            P("dev", "cam", None, None, None),
            P("dev", "cam", None, None, None),
            P("dev", None, None, None),
        ),
        check_vma=False,
    )
```

```python
import math

import jax
import jax.numpy as jnp
from jax import lax
from jax.experimental import pallas as pl
from jax.experimental.pallas import tpu as pltpu
from jax.sharding import PartitionSpec as P

TSIDE = 16
PIX = TSIDE * TSIDE
LANES = 128
PROJ = 9
FIELDS = 59
QUARTER = 15
PIECE = 16

LOSS_WEIGHT = 256.0
RATE = 0.01
BETA_FIRST = 0.9
BETA_SECOND = 0.999
EPSILON = 1e-08
SHRINK = math.log(1.6)
LOG2E = math.log2(math.e)

VMEM = pl.BlockSpec(memory_space=pltpu.VMEM)
SMEM = pl.BlockSpec(memory_space=pltpu.SMEM)
PARAMS = pltpu.CompilerParams(vmem_limit_bytes=40 * 1024 * 1024)


def softplus(values):
    return jnp.maximum(values, 0.0) + jnp.log1p(jnp.exp(-jnp.abs(values)))


def sigmoid(values):
    return 1.0 / (1.0 + jnp.exp(-values))


def project_kernel(proj_ref, send_ref, params_ref, out_ref, raw_ref, feat_ref):
    centre, spread = 0.5 * TSIDE, 0.375 * TSIDE
    fields = params_ref.shape[0]
    for camera in range(2):
        raw = [None] * PROJ
        for field in range(fields):
            row = params_ref[field]
            for p in range(PROJ):
                term = proj_ref[camera, p, field] * row
                raw[p] = term if field == 0 else raw[p] + term
        for p in range(PROJ):
            raw_ref[camera * PROJ + p] = raw[p]
    for camera in range(2):
        first = camera * PROJ
        raw = [raw_ref[first + p] for p in range(PROJ)]
        conic_a = 0.02 + 0.1 * softplus(raw[2])
        conic_c = 0.02 + 0.1 * softplus(raw[4])
        feat_ref[first + 0] = centre + spread * jnp.tanh(raw[0])
        feat_ref[first + 1] = centre + spread * jnp.tanh(raw[1])
        feat_ref[first + 2] = conic_a
        feat_ref[first + 3] = 0.9 * jnp.sqrt(conic_a * conic_c) * jnp.tanh(raw[3])
        feat_ref[first + 4] = conic_c
        feat_ref[first + 5] = 0.99 * sigmoid(raw[5] - 6.0)
        for p in range(6, PROJ):
            feat_ref[first + p] = sigmoid(raw[p])

    def place(j, unused):
        for camera in range(2):
            block = send_ref[camera, j]
            for p in range(PROJ):
                out_ref[j, p, pl.ds(camera, 1), :] = feat_ref[camera * PROJ + p, pl.ds(block, 1), :]
        return unused

    lax.fori_loop(0, out_ref.shape[0], place, 0, unroll=4)


SPLITS = 2
GROUP = 128


def split_parts(values):
    parts = []
    for at in range(SPLITS):
        part = values.astype(jnp.bfloat16)
        parts.append(part)
        if at < SPLITS - 1:
            values = values - part.astype(jnp.float32)
    return parts


def render_kernel(
    slot_ref,
    count_ref,
    recv_ref,
    target_ref,
    back_ref,
    image_ref,
    alpha_ref,
    reach_ref,
    shade_ref,
    part_ref,
    before_ref,
    behind_ref,
    colour_ref,
    carry_ref,
):
    lane = lax.broadcasted_iota(jnp.int32, (GROUP, LANES), 1)
    column = lax.broadcasted_iota(jnp.int32, (TSIDE, LANES), 0).astype(jnp.float32) + 0.5
    row = lax.broadcasted_iota(jnp.int32, (LANES, 2 * LANES), 0)
    col = lax.broadcasted_iota(jnp.int32, (LANES, 2 * LANES), 1)
    earlier = jnp.where((row < col) | (col >= LANES), 1.0, 0.0).astype(jnp.bfloat16)
    later = jnp.where((row > col) | (col >= LANES), 1.0, 0.0).astype(jnp.bfloat16)
    for at in range(SPLITS):
        before_ref[at * LANES : (at + 1) * LANES] = earlier
        behind_ref[at * LANES : (at + 1) * LANES] = later
    back_ref[...] = jnp.zeros(back_ref.shape, jnp.float32)
    image_ref[...] = jnp.zeros(image_ref.shape, jnp.float32)

    def tile(index, unused):
        camera = index // 2
        which = index % 2
        count = count_ref[camera, which]
        pairs = (count + 1) // 2

        def slot_at(k):
            return slot_ref[camera, which, jnp.minimum(k, count - 1)]

        def feature(slot, p):
            return recv_ref[slot, p, pl.ds(camera, 1), :]

        carry_ref[...] = jnp.zeros(carry_ref.shape, jnp.float32)

        def forward(pair, unused):
            for e in range(2):
                k = pair * 2 + e
                slot = slot_at(k)
                opacity = jnp.where(k < count, feature(slot, 5), 0.0)
                off_x = column - feature(slot, 0)
                mean_y = feature(slot, 1)
                half_a = (-0.5 * LOG2E) * feature(slot, 2)
                full_b = -LOG2E * feature(slot, 3)
                half_c = (-0.5 * LOG2E) * feature(slot, 4)
                square_x = half_a * off_x * off_x
                for y in range(TSIDE):
                    off_y = (y + 0.5) - mean_y
                    alpha = opacity * jnp.exp2(square_x + ((full_b * off_y) * off_x + half_c * off_y * off_y))
                    rows = slice(y * TSIDE, (y + 1) * TSIDE)
                    alpha_ref[k, rows] = alpha
                    for at, part in enumerate(split_parts(jnp.log(1.0 - alpha))):
                        part_ref[pair, e * PIX + y * TSIDE : e * PIX + (y + 1) * TSIDE, at * LANES : (at + 1) * LANES] = part
            sums = jnp.dot(part_ref[pair], before_ref[...], preferred_element_type=jnp.float32)
            carry = carry_ref[...]
            for e in range(2):
                reach_ref[pair * 2 + e] = jnp.exp(carry + sums[e * PIX : (e + 1) * PIX, :LANES])
                carry = carry + sums[e * PIX : (e + 1) * PIX, LANES:]
            carry_ref[...] = carry
            return unused

        lax.fori_loop(0, pairs, forward, 0)

        for group in range(PIX // GROUP):
            rows = slice(group * GROUP, (group + 1) * GROUP)

            def compose(pair, totals):
                totals = list(totals)
                for e in range(2):
                    k = pair * 2 + e
                    slot = slot_at(k)
                    weights = alpha_ref[k, rows] * reach_ref[k, rows]
                    for c in range(3):
                        totals[c] = totals[c] + feature(slot, 6 + c) * weights
                return tuple(totals)

            zero = jnp.zeros((GROUP, LANES), jnp.float32)
            totals = lax.fori_loop(0, pairs, compose, (zero, zero, zero))
            cotangent = []
            picture = image_ref[rows]
            for c in range(3):
                colour = jnp.sum(totals[c], axis=1, keepdims=True)
                place = index * 3 + c
                picture = jnp.where(lane == place, colour, picture)
                target = pltpu.roll(target_ref[rows], LANES - place, 1)[:, :1]
                cotangent.append(jnp.broadcast_to(LOSS_WEIGHT * (colour - target), (GROUP, LANES)))
            image_ref[rows] = picture

            def shade_all(pair, unused):
                for e in range(2):
                    k = pair * 2 + e
                    slot = slot_at(k)
                    weights = alpha_ref[k, rows] * reach_ref[k, rows]
                    shade = feature(slot, 6) * cotangent[0]
                    for c in range(1, 3):
                        shade = shade + feature(slot, 6 + c) * cotangent[c]
                    shade = shade * weights
                    shade_ref[k, rows] = shade
                    for at, part in enumerate(split_parts(shade)):
                        part_ref[pair, e * PIX + group * GROUP : e * PIX + (group + 1) * GROUP, at * LANES : (at + 1) * LANES] = part
                    for c in range(3):
                        piece = jnp.sum((cotangent[c] * weights).reshape(GROUP // 8, 8, LANES), axis=0)
                        colour_ref[k, c] = piece if group == 0 else colour_ref[k, c] + piece
                return unused

            lax.fori_loop(0, pairs, shade_all, 0)

        carry_ref[...] = jnp.zeros(carry_ref.shape, jnp.float32)

        def backward(step, unused):
            pair = pairs - 1 - step
            sums = jnp.dot(part_ref[pair], behind_ref[...], preferred_element_type=jnp.float32)
            for e in (1, 0):
                k = pair * 2 + e
                slot = slot_at(k)
                off_x = column - feature(slot, 0)
                mean_y = feature(slot, 1)
                plain, first_y, second_y = None, None, None
                for y in range(TSIDE):
                    rows = slice(y * TSIDE, (y + 1) * TSIDE)
                    inside = slice(e * PIX + y * TSIDE, e * PIX + (y + 1) * TSIDE)
                    carry = carry_ref[rows]
                    alpha = alpha_ref[k, rows]
                    keep = 1.0 - alpha
                    inverse = pl.reciprocal(keep, approx=True)
                    inverse = inverse * (2.0 - keep * inverse)
                    pull = shade_ref[k, rows] - (carry + sums[inside, :LANES]) * (alpha * inverse)
                    carry_ref[rows] = carry + sums[inside, LANES:]
                    off_y = (y + 0.5) - mean_y
                    once = off_y * pull
                    twice = off_y * once
                    plain = pull if y == 0 else plain + pull
                    first_y = once if y == 0 else first_y + once
                    second_y = twice if y == 0 else second_y + twice

                def total(values):
                    return jnp.sum(values, axis=0, keepdims=True)

                along_x = off_x * plain
                sum_x = total(along_x)
                sum_y = total(first_y)
                conic_a, conic_b, conic_c = feature(slot, 2), feature(slot, 3), feature(slot, 4)
                grads = [
                    conic_a * sum_x + conic_b * sum_y,
                    conic_b * sum_x + conic_c * sum_y,
                    -0.5 * total(off_x * along_x),
                    -total(off_x * first_y),
                    -0.5 * total(second_y),
                    total(plain),
                ]
                for c in range(3):
                    grads.append(total(colour_ref[k, c]))
                for p in range(PROJ):
                    spot = (slot, p, pl.ds(camera, 1), slice(None))
                    back_ref[spot] = back_ref[spot] + grads[p]
            return unused

        lax.fori_loop(0, pairs, backward, 0)
        return unused

    lax.fori_loop(0, 4, tile, 0)


RENDER_SCRATCH = [
    pltpu.VMEM((8, PIX, LANES), jnp.float32),
    pltpu.VMEM((8, PIX, LANES), jnp.float32),
    pltpu.VMEM((8, PIX, LANES), jnp.float32),
    pltpu.VMEM((4, 2 * PIX, SPLITS * LANES), jnp.bfloat16),
    pltpu.VMEM((SPLITS * LANES, 2 * LANES), jnp.bfloat16),
    pltpu.VMEM((SPLITS * LANES, 2 * LANES), jnp.bfloat16),
    pltpu.VMEM((8, 3, 8, LANES), jnp.float32),
    pltpu.VMEM((PIX, LANES), jnp.float32),
]


def collect_kernel(send_ref, back_ref, raw_ref, out_ref, acc_ref):
    acc_ref[...] = jnp.zeros(acc_ref.shape, jnp.float32)

    def gather(j, unused):
        for camera in range(2):
            block = send_ref[camera, j]
            for p in range(PROJ):
                spot = (camera * PROJ + p, pl.ds(block, 1), slice(None))
                acc_ref[spot] = acc_ref[spot] + back_ref[j, p, pl.ds(camera, 1), :]
        return unused

    lax.fori_loop(0, back_ref.shape[0], gather, 0)
    spread = 0.375 * TSIDE
    for camera in range(2):
        first = camera * PROJ
        raw = [raw_ref[first + p] for p in range(PROJ)]
        grad = [acc_ref[first + p] for p in range(PROJ)]
        conic_a = 0.02 + 0.1 * softplus(raw[2])
        conic_c = 0.02 + 0.1 * softplus(raw[4])
        root = 0.9 * jnp.sqrt(conic_a * conic_c)
        turn = jnp.tanh(raw[3])
        from_b = 0.5 * grad[3] * root * turn
        tan_x, tan_y = jnp.tanh(raw[0]), jnp.tanh(raw[1])
        result = [
            grad[0] * spread * (1.0 - tan_x * tan_x),
            grad[1] * spread * (1.0 - tan_y * tan_y),
            (grad[2] + from_b / conic_a) * 0.1 * sigmoid(raw[2]),
            grad[3] * root * (1.0 - turn * turn),
            (grad[4] + from_b / conic_c) * 0.1 * sigmoid(raw[4]),
            grad[5] * (1.0 - sigmoid(raw[5] - 6.0)),
        ]
        for p in range(6, PROJ):
            shade = sigmoid(raw[p])
            result.append(grad[p] * shade * (1.0 - shade))
        for p in range(PROJ):
            out_ref[first + p] = result[p]


def pack_kernel(place_ref, first_ref, second_ref, *out_refs):
    for ahead, out_ref in enumerate(out_refs):
        quarter = lax.rem(place_ref[0] + ahead, 4)
        for field in range(QUARTER):
            at = jnp.minimum(quarter * QUARTER + field, FIELDS - 1)
            out_ref[0, field] = first_ref[at]
            out_ref[1, field] = second_ref[at]


def step_of(first, second, old, grad):
    new_first = BETA_FIRST * first + (1.0 - BETA_FIRST) * grad
    new_second = BETA_SECOND * second + (1.0 - BETA_SECOND) * grad * grad
    return new_first, new_second, old - RATE * new_first / (jnp.sqrt(new_second) + EPSILON)


def pull_rows(own_ref, before_ref, after_ref, low_ref, high_ref, blocks):
    for row in range(2 * PROJ):
        yield 0, row, own_ref[row, blocks, :]
        yield 1, row, before_ref[row, blocks, :]
        yield 2, row, after_ref[row, blocks, :]
        yield 3, row, low_ref[row, blocks, :] if row < PROJ else high_ref[row - PROJ, blocks, :]


def quarter_kernel(
    place_ref,
    block_ref,
    live_ref,
    proj_0,
    proj_1,
    proj_2,
    proj_3,
    own_ref,
    before_ref,
    after_ref,
    low_ref,
    high_ref,
    params_ref,
    moment_0,
    moment_1,
    moment_2,
    moment_3,
    new_ref,
    parents_ref,
    grad_ref,
):
    projs = (proj_0, proj_1, proj_2, proj_3)
    owned = params_ref.shape[1]
    share = moment_0.shape[2]
    base = place_ref[0] * QUARTER
    width = 5
    for low in range(0, QUARTER, width):
        grads = [None] * width
        for source, row, value in pull_rows(own_ref, before_ref, after_ref, low_ref, high_ref, slice(None)):
            for at in range(width):
                field = jnp.minimum(base + low + at, FIELDS - 1)
                term = projs[source][row // PROJ, row % PROJ, field] * value
                grads[at] = term if grads[at] is None else grads[at] + term
        for at in range(width):
            grad_ref[low + at] = grads[at]
    for ahead, moment_ref in enumerate((moment_0, moment_1, moment_2, moment_3)):
        start = pl.multiple_of(lax.rem(place_ref[0] + (4 - ahead), 4) * share, share)
        blocks = pl.ds(start, share)
        for field in range(QUARTER):
            old = params_ref[jnp.minimum(base + field, FIELDS - 1), blocks, :]
            new = step_of(moment_ref[0, field], moment_ref[1, field], old, grad_ref[field, blocks, :])[2]
            new_ref[field, blocks, :] = new

    def place(j, unused):
        block = block_ref[0, j]
        for field in range(QUARTER):
            parents_ref[j, pl.ds(field, 1), :] = new_ref[field, pl.ds(block, 1), :]
        live = live_ref[0, j].astype(jnp.float32)
        parents_ref[j, pl.ds(QUARTER, 1), :] = jnp.full((1, LANES), live, jnp.float32)
        return unused

    lax.fori_loop(0, parents_ref.shape[0], place, 0, unroll=4)


def moments_kernel(
    place_ref,
    proj_0,
    proj_1,
    proj_2,
    proj_3,
    own_ref,
    before_ref,
    after_ref,
    low_ref,
    high_ref,
    first_ref,
    second_ref,
    new_first_ref,
    new_second_ref,
):
    projs = (proj_0, proj_1, proj_2, proj_3)
    share = first_ref.shape[1]
    blocks = pl.ds(pl.multiple_of(place_ref[0] * share, share), share)
    width = 12
    for low in range(0, FIELDS, width):
        fields = range(low, min(low + width, FIELDS))
        grads = [None] * len(fields)
        for source, row, value in pull_rows(own_ref, before_ref, after_ref, low_ref, high_ref, blocks):
            for at, field in enumerate(fields):
                term = projs[source][row // PROJ, row % PROJ, field] * value
                grads[at] = term if grads[at] is None else grads[at] + term
        for at, field in enumerate(fields):
            first, second, unused = step_of(first_ref[field], second_ref[field], 0.0, grads[at])
            new_first_ref[field] = first
            new_second_ref[field] = second


def assemble_kernel(place_ref, own_ref, before_ref, after_ref, low_ref, high_ref, out_ref):
    for field in range(QUARTER - 1, -1, -1):
        half = low_ref.shape[0]
        far = low_ref[field] if field < half else high_ref[field - half]
        rows = ((0, own_ref[field]), (3, before_ref[field]), (1, after_ref[field]), (2, far))
        for ahead, value in rows:
            quarter = lax.rem(place_ref[0] + ahead, 4)
            out_ref[jnp.minimum(quarter * QUARTER + field, FIELDS - 1)] = value


def children_kernel(place_ref, own_ref, before_ref, after_ref, far_low_ref, far_high_ref, out_ref):
    step = pl.program_id(0)
    half = pl.num_programs(0) // 2

    def fill(ref, offset):
        quarter = lax.rem(place_ref[0] + offset, 4)
        first = quarter == 0

        def one(j, unused):
            live = ref[j, pl.ds(QUARTER, 1), :] > 0.5
            rows = [ref[j, pl.ds(field, 1), :] for field in range(QUARTER)]
            for field in range(QUARTER):
                at = jnp.minimum(quarter * QUARTER + field, FIELDS - 1)
                if field < 3:
                    off = jnp.where(first, 0.5 * jnp.exp(rows[field + 3] - 1.0), 0.0)
                    out_ref[j, at, pl.ds(0, 1), :] = jnp.where(live, rows[field] + off, 0.0)
                    out_ref[j, at, pl.ds(1, 1), :] = jnp.where(live, rows[field] - off, 0.0)
                else:
                    row = rows[field]
                    if field < 6:
                        row = row - jnp.where(first, SHRINK, 0.0)
                    out_ref[j, at] = jnp.broadcast_to(jnp.where(live, row, 0.0), (2, LANES))
            return unused

        lax.fori_loop(0, out_ref.shape[0], one, 0, unroll=4)

    fill(own_ref, 0)
    fill(before_ref, 3)
    fill(after_ref, 1)

    @pl.when(step < half)
    def _():
        fill(far_low_ref, 2)

    @pl.when(step >= half)
    def _():
        fill(far_high_ref, 2)


def shape(*dims):
    return jax.ShapeDtypeStruct(dims, jnp.float32)


def shift_by(values, distance):
    size = lax.axis_size("cam")
    return lax.ppermute(values, "cam", [(i, (i + distance) % size) for i in range(size)])


def ring_gather(values, half):
    before = shift_by(values, 1)
    after = shift_by(values, 3)
    return values, before, after, shift_by(before[:half], 1), shift_by(after[half:], 3)


def call(kernel, inputs, outputs, scratch=(), name=None):
    where = [SMEM if kind == "s" else VMEM for kind, unused in inputs]
    several = isinstance(outputs, tuple)
    return pl.pallas_call(
        kernel,
        out_shape=outputs,
        in_specs=where,
        out_specs=tuple(VMEM for unused in outputs) if several else VMEM,
        scratch_shapes=list(scratch),
        compiler_params=PARAMS,
        name=name,
    )(*[value for unused, value in inputs])


def body(
    params,
    moment_first,
    moment_second,
    cam_proj,
    send_block,
    tile_slot,
    tile_count,
    targets,
    split_block,
    split_live,
):
    owned = params.shape[0]
    owners = split_block.shape[1]
    groups = lax.axis_size("cam")
    share = owned // groups
    place = lax.axis_index("cam").astype(jnp.int32).reshape(1)
    by_field = params.transpose(1, 0, 2)
    send = send_block.reshape(2, owners)
    wire = shape(owners, PROJ, 2, LANES)
    rows = shape(2 * PROJ, owned, LANES)
    plane = pltpu.VMEM((2 * PROJ, owned, LANES), jnp.float32)

    def s(value):
        return ("s", value)

    def v(value):
        return ("v", value)

    outgoing, raw = call(project_kernel, [s(cam_proj), s(send), v(by_field)], (wire, rows), [plane], "project")
    received = lax.all_to_all(outgoing, "dev", split_axis=0, concat_axis=0, tiled=True)

    first = moment_first.reshape(share, FIELDS, LANES).transpose(1, 0, 2)
    second = moment_second.reshape(share, FIELDS, LANES).transpose(1, 0, 2)
    packed = call(
        pack_kernel, [s(place), v(first), v(second)], tuple(shape(2, QUARTER, share, LANES) for unused in range(4)), (), "pack"
    )
    moments = [packed[0]] + [shift_by(packed[ahead], ahead) for ahead in range(1, 4)]
    projs = [cam_proj, shift_by(cam_proj, 1), shift_by(cam_proj, 3), shift_by(cam_proj, 2)]
    target = jnp.pad(targets.reshape(12, PIX).T, ((0, 0), (0, LANES - 12)))
    received, target, moments, projs = lax.optimization_barrier((received, target, moments, projs))

    returning, pictures = call(
        render_kernel,
        [s(tile_slot), s(tile_count), v(received), v(target)],
        (wire, shape(PIX, LANES)),
        RENDER_SCRATCH,
        "render",
    )
    returned = lax.all_to_all(returning, "dev", split_axis=0, concat_axis=0, tiled=True)
    images = pictures[:, :12].T.reshape(targets.shape)
    pulls = call(collect_kernel, [s(send), v(returned), v(raw)], rows, [plane], "collect")
    pulls = [v(value) for value in ring_gather(pulls, PROJ)]
    projs = [s(value) for value in projs]
    fresh, parents = call(
        quarter_kernel,
        [s(place), s(split_block), s(split_live)] + projs + pulls + [v(by_field)] + [v(value) for value in moments],
        (shape(QUARTER, owned, LANES), shape(owners, PIECE, LANES)),
        [pltpu.VMEM((QUARTER, owned, LANES), jnp.float32)],
        "quarter",
    )
    parents = lax.all_to_all(parents, "dev", split_axis=0, concat_axis=0, tiled=True)
    own = shape(FIELDS, share, LANES)
    new_first, new_second = call(moments_kernel, [s(place)] + projs + pulls + [v(first), v(second)], (own, own), (), "moments")
    fresh = [v(value) for value in ring_gather(fresh, QUARTER // 2)]
    new_params = call(assemble_kernel, [s(place)] + fresh, shape(FIELDS, owned, LANES), (), "assemble")
    parents, new_params, new_first, new_second = lax.optimization_barrier((parents, new_params, new_first, new_second))
    pieces = ring_gather(parents, owners // 2)
    batch = 8
    steps = owners // batch

    def block(index):
        return pl.BlockSpec((batch, PIECE, LANES), index)

    children = pl.pallas_call(
        children_kernel,
        grid=(steps,),
        out_shape=shape(owners, FIELDS, 2, LANES),
        in_specs=[
            SMEM,
            block(lambda i: (i, 0, 0)),
            block(lambda i: (i, 0, 0)),
            block(lambda i: (i, 0, 0)),
            block(lambda i: (jnp.minimum(i, steps // 2 - 1), 0, 0)),
            block(lambda i: (jnp.maximum(i - steps // 2, 0), 0, 0)),
        ],
        out_specs=pl.BlockSpec((batch, FIELDS, 2, LANES), lambda i: (i, 0, 0, 0)),
        compiler_params=PARAMS,
        name="children",
    )(place, *pieces)

    def back(values):
        return values.transpose(1, 0, 2).reshape(moment_first.shape)

    return (
        images,
        new_params.transpose(1, 0, 2),
        back(new_first),
        back(new_second),
        children.transpose(0, 2, 1, 3),
    )


def solution(mesh):
    placed = (
        P("dev", None, None),
        P("dev", "cam", None, None, None),
        P("dev", "cam", None, None, None),
        P("cam", None, None),
        P("cam", "dev", None, None),
        P("cam", "dev", None),
        P("cam", "dev"),
        P("cam", "dev", None, None),
        P("dev", None),
        P("dev", None),
    )
    return jax.shard_map(
        body,
        mesh=mesh,
        in_specs=placed,
        out_specs=(
            P("cam", "dev", None, None),
            P("dev", None, None),
            P("dev", "cam", None, None, None),
            P("dev", "cam", None, None, None),
            P("dev", None, None, None),
        ),
        check_vma=False,
    )
```

```python
import math

import jax
import jax.numpy as jnp
from jax import lax
from jax.experimental import pallas as pl
from jax.experimental.pallas import tpu as pltpu
from jax.sharding import PartitionSpec as P

TSIDE = 16
PIX = TSIDE * TSIDE
LANES = 128
PROJ = 9
KMAX = 8
FIELDS = 59
QUARTER = 15
WIDTH = 5
PIECE = 16

LOSS_WEIGHT = 256.0
RATE = 0.01
BETA_FIRST = 0.9
BETA_SECOND = 0.999
EPSILON = 1e-08
SHRINK = math.log(1.6)
LOG2E = math.log2(math.e)

VMEM = pl.BlockSpec(memory_space=pltpu.VMEM)
SMEM = pl.BlockSpec(memory_space=pltpu.SMEM)
HBM = pl.BlockSpec(memory_space=pltpu.HBM)
PARAMS = pltpu.CompilerParams(vmem_limit_bytes=40 * 1024 * 1024)


def softplus(values):
    return jnp.maximum(values, 0.0) + jnp.log1p(jnp.exp(-jnp.abs(values)))


def sigmoid(values):
    return 1.0 / (1.0 + jnp.exp(-values))


def project_kernel(proj_in, send_in, params_ref, out_ref, raw_ref, held_ref, feat_ref, proj_ref, send_ref, sems):
    centre, spread = 0.5 * TSIDE, 0.375 * TSIDE
    copies = []
    for part, low in enumerate(range(0, FIELDS, QUARTER)):
        rows = pl.ds(low, min(QUARTER, FIELDS - low))
        copies.append(pltpu.make_async_copy(params_ref.at[rows], held_ref.at[rows], sems.at[part]))
        copies[-1].start()
    lists = pltpu.make_async_copy(send_in, send_ref, sems.at[4])
    weights = pltpu.make_async_copy(proj_in, proj_ref, sems.at[5])
    weights.start()
    lists.start()
    weights.wait()
    lists.wait()
    for part, copy in enumerate(copies):
        copy.wait()
        low = part * QUARTER
        for camera in range(2):
            raw = [None] * PROJ if part == 0 else [raw_ref[camera * PROJ + p] for p in range(PROJ)]
            for field in range(low, min(low + QUARTER, FIELDS)):
                row = held_ref[field]
                for p in range(PROJ):
                    term = proj_ref[p, camera, field] * row
                    raw[p] = term if field == 0 else raw[p] + term
            for p in range(PROJ):
                raw_ref[camera * PROJ + p] = raw[p]
    for camera in range(2):
        first = camera * PROJ
        raw = [raw_ref[first + p] for p in range(PROJ)]
        conic_a = 0.02 + 0.1 * softplus(raw[2])
        conic_c = 0.02 + 0.1 * softplus(raw[4])
        feat_ref[first + 0] = centre + spread * jnp.tanh(raw[0])
        feat_ref[first + 1] = centre + spread * jnp.tanh(raw[1])
        feat_ref[first + 2] = conic_a
        feat_ref[first + 3] = 0.9 * jnp.sqrt(conic_a * conic_c) * jnp.tanh(raw[3])
        feat_ref[first + 4] = conic_c
        feat_ref[first + 5] = 0.99 * sigmoid(raw[5] - 6.0)
        for p in range(6, PROJ):
            feat_ref[first + p] = sigmoid(raw[p])

    def place(j, unused):
        for camera in range(2):
            block = send_ref[camera, j]
            for p in range(PROJ):
                out_ref[j, p, pl.ds(camera, 1), :] = feat_ref[camera * PROJ + p, pl.ds(block, 1), :]
        return unused

    lax.fori_loop(0, out_ref.shape[0], place, 0, unroll=4)


SPLITS = 2


def split_parts(values):
    parts = []
    for at in range(SPLITS):
        part = values.astype(jnp.bfloat16)
        parts.append(part)
        if at < SPLITS - 1:
            values = values - part.astype(jnp.float32)
    return parts


def render_kernel(
    plan_ref,
    recv_ref,
    target_ref,
    back_ref,
    image_ref,
    alpha_ref,
    weight_ref,
    shade_ref,
    part_ref,
    before_ref,
    behind_ref,
    acc_ref,
    carry_ref,
):
    lane = lax.broadcasted_iota(jnp.int32, (PIX, LANES), 1)
    column = lax.broadcasted_iota(jnp.int32, (TSIDE, LANES), 0).astype(jnp.float32) + 0.5
    row = lax.broadcasted_iota(jnp.int32, (LANES, 2 * LANES), 0)
    col = lax.broadcasted_iota(jnp.int32, (LANES, 2 * LANES), 1)
    earlier = jnp.where((row < col) | (col >= LANES), 1.0, 0.0).astype(jnp.bfloat16)
    later = jnp.where((row > col) | (col >= LANES), 1.0, 0.0).astype(jnp.bfloat16)
    for at in range(SPLITS):
        before_ref[at * LANES : (at + 1) * LANES] = earlier
        behind_ref[at * LANES : (at + 1) * LANES] = later
    back_ref[...] = jnp.zeros(back_ref.shape, jnp.float32)
    image_ref[...] = jnp.zeros(image_ref.shape, jnp.float32)

    def tile(index, unused):
        camera = index // 2
        which = index % 2
        count = plan_ref[camera, 2 * KMAX + which]
        pairs = (count + 1) // 2

        def slot_at(k):
            return plan_ref[camera, which * KMAX + jnp.minimum(k, count - 1)]

        def feature(slot, p):
            return recv_ref[slot, p, pl.ds(camera, 1), :]

        def put_parts(start, values):
            for at, part in enumerate(split_parts(values)):
                part_ref[start : start + values.shape[0], at * LANES : (at + 1) * LANES] = part

        carry_ref[...] = jnp.zeros(carry_ref.shape, jnp.float32)
        acc_ref[...] = jnp.zeros(acc_ref.shape, jnp.float32)

        def forward(pair, unused):
            slots = [slot_at(pair * 2 + e) for e in range(2)]
            for e in range(2):
                k = pair * 2 + e
                slot = slots[e]
                opacity = jnp.where(k < count, feature(slot, 5), 0.0)
                off_x = column - feature(slot, 0)
                mean_y = feature(slot, 1)
                half_a = (-0.5 * LOG2E) * feature(slot, 2)
                full_b = -LOG2E * feature(slot, 3)
                half_c = (-0.5 * LOG2E) * feature(slot, 4)
                square_x = half_a * off_x * off_x
                for y in range(TSIDE):
                    off_y = (y + 0.5) - mean_y
                    alpha = opacity * jnp.exp2(square_x + ((full_b * off_y) * off_x + half_c * off_y * off_y))
                    alpha_ref[k, y * TSIDE : (y + 1) * TSIDE] = alpha
                    put_parts(e * PIX + y * TSIDE, jnp.log(1.0 - alpha))
            sums = jnp.dot(part_ref[...], before_ref[...], preferred_element_type=jnp.float32)
            colours = [[feature(slots[e], 6 + c) for c in range(3)] for e in range(2)]
            for y in range(TSIDE):
                rows = slice(y * TSIDE, (y + 1) * TSIDE)
                next_rows = slice(PIX + y * TSIDE, PIX + (y + 1) * TSIDE)
                carry = carry_ref[rows]
                weights = [alpha_ref[pair * 2, rows] * jnp.exp(carry + sums[rows, :LANES])]
                carry = carry + sums[rows, LANES:]
                weights.append(alpha_ref[pair * 2 + 1, rows] * jnp.exp(carry + sums[next_rows, :LANES]))
                carry_ref[rows] = carry + sums[next_rows, LANES:]
                weight_ref[pair * 2, rows] = weights[0]
                weight_ref[pair * 2 + 1, rows] = weights[1]
                for c in range(3):
                    acc_ref[c, rows] = acc_ref[c, rows] + (colours[0][c] * weights[0] + colours[1][c] * weights[1])
            return unused

        lax.fori_loop(0, pairs, forward, 0)
        for c in range(3):
            place = index * 3 + c
            put_parts(0, acc_ref[c])
            colour = jnp.dot(part_ref[:PIX], before_ref[:, LANES:], preferred_element_type=jnp.float32)
            image_ref[...] = jnp.where(lane == place, colour, image_ref[...])
            acc_ref[c] = LOSS_WEIGHT * (colour - target_ref[place])
        carry_ref[...] = jnp.zeros(carry_ref.shape, jnp.float32)

        def backward(step, unused):
            pair = pairs - 1 - step
            slots = [slot_at(pair * 2 + e) for e in range(2)]
            colour_grads = []
            for e in range(2):
                k = pair * 2 + e
                colours = [feature(slots[e], 6 + c) for c in range(3)]
                sums_c = [None] * 3
                for y in range(TSIDE):
                    rows = slice(y * TSIDE, (y + 1) * TSIDE)
                    weights = weight_ref[k, rows]
                    cots = [acc_ref[c, rows] for c in range(3)]
                    shade = (colours[0] * cots[0] + colours[1] * cots[1] + colours[2] * cots[2]) * weights
                    shade_ref[e, rows] = shade
                    put_parts(e * PIX + y * TSIDE, shade)
                    for c in range(3):
                        term = cots[c] * weights
                        sums_c[c] = term if y == 0 else sums_c[c] + term
                colour_grads.append(sums_c)
            sums = jnp.dot(part_ref[...], behind_ref[...], preferred_element_type=jnp.float32)
            for e in (1, 0):
                k = pair * 2 + e
                slot = slots[e]
                off_x = column - feature(slot, 0)
                mean_y = feature(slot, 1)
                plain, first_y, second_y = None, None, None
                for y in range(TSIDE):
                    rows = slice(y * TSIDE, (y + 1) * TSIDE)
                    inside = slice(e * PIX + y * TSIDE, e * PIX + (y + 1) * TSIDE)
                    carry = carry_ref[rows]
                    alpha = alpha_ref[k, rows]
                    keep = 1.0 - alpha
                    inverse = pl.reciprocal(keep, approx=True)
                    inverse = inverse * (2.0 - keep * inverse)
                    pull = shade_ref[e, rows] - (carry + sums[inside, :LANES]) * (alpha * inverse)
                    carry_ref[rows] = carry + sums[inside, LANES:]
                    off_y = (y + 0.5) - mean_y
                    once = off_y * pull
                    twice = off_y * once
                    plain = pull if y == 0 else plain + pull
                    first_y = once if y == 0 else first_y + once
                    second_y = twice if y == 0 else second_y + twice

                def total(values):
                    return jnp.sum(values, axis=0, keepdims=True)

                along_x = off_x * plain
                sum_x = total(along_x)
                sum_y = total(first_y)
                conic_a, conic_b, conic_c = feature(slot, 2), feature(slot, 3), feature(slot, 4)
                grads = [
                    conic_a * sum_x + conic_b * sum_y,
                    conic_b * sum_x + conic_c * sum_y,
                    -0.5 * total(off_x * along_x),
                    -total(off_x * first_y),
                    -0.5 * total(second_y),
                    total(plain),
                ] + [total(values) for values in colour_grads[e]]
                for p in range(PROJ):
                    spot = (slot, p, pl.ds(camera, 1), slice(None))
                    back_ref[spot] = back_ref[spot] + grads[p]
            return unused

        lax.fori_loop(0, pairs, backward, 0)
        return unused

    lax.fori_loop(0, 4, tile, 0)


RENDER_SCRATCH = [
    pltpu.VMEM((8, PIX, LANES), jnp.float32),
    pltpu.VMEM((8, PIX, LANES), jnp.float32),
    pltpu.VMEM((2, PIX, LANES), jnp.float32),
    pltpu.VMEM((2 * PIX, SPLITS * LANES), jnp.bfloat16),
    pltpu.VMEM((SPLITS * LANES, 2 * LANES), jnp.bfloat16),
    pltpu.VMEM((SPLITS * LANES, 2 * LANES), jnp.bfloat16),
    pltpu.VMEM((3, PIX, LANES), jnp.float32),
    pltpu.VMEM((PIX, LANES), jnp.float32),
]


def collect_kernel(send_ref, back_ref, raw_ref, out_ref, acc_ref):
    acc_ref[...] = jnp.zeros(acc_ref.shape, jnp.float32)

    def gather(j, unused):
        for camera in range(2):
            block = send_ref[camera, j]
            for p in range(PROJ):
                spot = (camera * PROJ + p, pl.ds(block, 1), slice(None))
                acc_ref[spot] = acc_ref[spot] + back_ref[j, p, pl.ds(camera, 1), :]
        return unused

    lax.fori_loop(0, back_ref.shape[0], gather, 0)
    spread = 0.375 * TSIDE
    for camera in range(2):
        first = camera * PROJ
        raw = [raw_ref[first + p] for p in range(PROJ)]
        grad = [acc_ref[first + p] for p in range(PROJ)]
        conic_a = 0.02 + 0.1 * softplus(raw[2])
        conic_c = 0.02 + 0.1 * softplus(raw[4])
        root = 0.9 * jnp.sqrt(conic_a * conic_c)
        turn = jnp.tanh(raw[3])
        from_b = 0.5 * grad[3] * root * turn
        tan_x, tan_y = jnp.tanh(raw[0]), jnp.tanh(raw[1])
        result = [
            grad[0] * spread * (1.0 - tan_x * tan_x),
            grad[1] * spread * (1.0 - tan_y * tan_y),
            (grad[2] + from_b / conic_a) * 0.1 * sigmoid(raw[2]),
            grad[3] * root * (1.0 - turn * turn),
            (grad[4] + from_b / conic_c) * 0.1 * sigmoid(raw[4]),
            grad[5] * (1.0 - sigmoid(raw[5] - 6.0)),
        ]
        for p in range(6, PROJ):
            shade = sigmoid(raw[p])
            result.append(grad[p] * shade * (1.0 - shade))
        for p in range(PROJ):
            out_ref[first + p] = result[p]


def pack_kernel(place_ref, first_ref, second_ref, *out_refs):
    for ahead, out_ref in enumerate(out_refs):
        quarter = lax.rem(place_ref[0] + ahead, 4)
        for field in range(QUARTER):
            at = jnp.minimum(quarter * QUARTER + field, FIELDS - 1)
            out_ref[0, field] = first_ref[at]
            out_ref[1, field] = second_ref[at]


def step_of(first, second, old, grad):
    new_first = BETA_FIRST * first + (1.0 - BETA_FIRST) * grad
    new_second = BETA_SECOND * second + (1.0 - BETA_SECOND) * grad * grad
    return new_first, new_second, old - RATE * new_first / (jnp.sqrt(new_second) + EPSILON)


def add_up(grads, proj_ref, source, low_ref, high_ref, blocks, fields):
    for row in range(2 * PROJ):
        value = low_ref[row, blocks, :] if row < PROJ else high_ref[row - PROJ, blocks, :]
        for at, field in enumerate(fields):
            term = proj_ref[row % PROJ, 2 * source + row // PROJ, field] * value
            grads[at] = term if grads[at] is None else grads[at] + term


def quarter_fields(place_ref, low):
    return [jnp.minimum(place_ref[0] * QUARTER + low + at, FIELDS - 1) for at in range(WIDTH)]


def near_kernel(place_ref, proj_ref, own_ref, before_low, before_high, after_low, after_high, grad_ref):
    for low in range(0, QUARTER, WIDTH):
        grads = [None] * WIDTH
        fields = quarter_fields(place_ref, low)
        own = (own_ref.at[pl.ds(0, PROJ)], own_ref.at[pl.ds(PROJ, PROJ)])
        for source, halves in enumerate((own, (before_low, before_high), (after_low, after_high))):
            add_up(grads, proj_ref, source, *halves, slice(None), fields)
        for at in range(WIDTH):
            grad_ref[low + at] = grads[at]


def quarter_kernel(
    place_ref,
    block_ref,
    live_ref,
    proj_ref,
    near_ref,
    far_low,
    far_high,
    params_ref,
    moment_0,
    moment_1,
    moment_2,
    moment_3,
    new_ref,
    parents_ref,
    grad_ref,
    held_ref,
    sem,
):
    share = moment_0.shape[2]
    base = place_ref[0] * QUARTER
    start = jnp.minimum(base, FIELDS - QUARTER)
    copy = pltpu.make_async_copy(params_ref.at[pl.ds(start, QUARTER)], held_ref, sem)
    copy.start()
    for low in range(0, QUARTER, WIDTH):
        grads = [near_ref[low + at] for at in range(WIDTH)]
        add_up(grads, proj_ref, 3, far_low, far_high, slice(None), quarter_fields(place_ref, low))
        for at in range(WIDTH):
            grad_ref[low + at] = grads[at]
    copy.wait()
    for ahead, moment_ref in enumerate((moment_0, moment_1, moment_2, moment_3)):
        blocks = pl.ds(pl.multiple_of(lax.rem(place_ref[0] + (4 - ahead), 4) * share, share), share)
        for field in range(QUARTER):
            old = held_ref[jnp.minimum(base - start + field, QUARTER - 1), blocks, :]
            new = step_of(moment_ref[0, field], moment_ref[1, field], old, grad_ref[field, blocks, :])[2]
            new_ref[field, blocks, :] = new

    def place(j, unused):
        block = block_ref[0, j]
        for field in range(QUARTER):
            parents_ref[j, pl.ds(field, 1), :] = new_ref[field, pl.ds(block, 1), :]
        live = live_ref[0, j].astype(jnp.float32)
        parents_ref[j, pl.ds(QUARTER, 1), :] = jnp.full((1, LANES), live, jnp.float32)
        return unused

    lax.fori_loop(0, parents_ref.shape[0], place, 0, unroll=4)


def moments_kernel(
    place_ref,
    proj_ref,
    own_ref,
    before_low,
    before_high,
    after_low,
    after_high,
    far_low,
    far_high,
    first_ref,
    second_ref,
    new_first_ref,
    new_second_ref,
):
    share = first_ref.shape[1]
    blocks = pl.ds(pl.multiple_of(place_ref[0] * share, share), share)
    own = (own_ref.at[pl.ds(0, PROJ)], own_ref.at[pl.ds(PROJ, PROJ)])
    sources = (own, (before_low, before_high), (after_low, after_high), (far_low, far_high))
    width = 12
    for low in range(0, FIELDS, width):
        fields = range(low, min(low + width, FIELDS))
        grads = [None] * len(fields)
        for source, halves in enumerate(sources):
            add_up(grads, proj_ref, source, *halves, blocks, fields)
        for at, field in enumerate(fields):
            first, second, unused = step_of(first_ref[field], second_ref[field], 0.0, grads[at])
            new_first_ref[field] = first
            new_second_ref[field] = second


def assemble_kernel(place_ref, own_ref, before_ref, after_ref, low_ref, high_ref, out_ref):
    for field in range(QUARTER - 1, -1, -1):
        half = low_ref.shape[0]
        far = low_ref[field] if field < half else high_ref[field - half]
        rows = ((0, own_ref[field]), (3, before_ref[field]), (1, after_ref[field]), (2, far))
        for ahead, value in rows:
            quarter = lax.rem(place_ref[0] + ahead, 4)
            out_ref[jnp.minimum(quarter * QUARTER + field, FIELDS - 1)] = value


def fill_children(ref, quarter, out_ref):
    first = quarter == 0

    def one(j, unused):
        live = jnp.broadcast_to(ref[j, pl.ds(QUARTER, 1), :], (2, LANES)) > 0.5
        sign = jnp.where(lax.broadcasted_iota(jnp.int32, (2, LANES), 0) == 0, 0.5, -0.5)
        rows = [jnp.broadcast_to(ref[j, pl.ds(field, 1), :], (2, LANES)) for field in range(QUARTER)]
        for field in range(QUARTER):
            row = rows[field]
            if field < 3:
                row = row + jnp.where(first, sign * jnp.exp(rows[field + 3] - 1.0), 0.0)
            elif field < 6:
                row = row - jnp.where(first, SHRINK, 0.0)
            out_ref[j, field] = jnp.where(live, row, 0.0)
        return unused

    lax.fori_loop(0, out_ref.shape[0], one, 0, unroll=8)


def near_children_kernel(place_ref, own_ref, before_low, before_high, after_low, after_high, out_ref):
    upper = pl.program_id(0) >= pl.num_programs(0) // 2
    piece = pl.program_id(1)

    @pl.when(piece == 0)
    def _():
        fill_children(own_ref, place_ref[0], out_ref)

    for at, ahead, low, high in ((1, 3, before_low, before_high), (2, 1, after_low, after_high)):

        @pl.when((piece == at) & jnp.logical_not(upper))
        def _():
            fill_children(low, lax.rem(place_ref[0] + ahead, 4), out_ref)

        @pl.when((piece == at) & upper)
        def _():
            fill_children(high, lax.rem(place_ref[0] + ahead, 4), out_ref)


def far_children_kernel(place_ref, far_low, far_high, near_ref, out_ref):
    upper = pl.program_id(0) >= pl.num_programs(0) // 2
    quarter = lax.rem(place_ref[0] + 2, 4)

    @pl.when(jnp.logical_not(upper))
    def _():
        fill_children(far_low, quarter, out_ref)

    @pl.when(upper)
    def _():
        fill_children(far_high, quarter, out_ref)


def shape(*dims):
    return jax.ShapeDtypeStruct(dims, jnp.float32)


def shift_by(values, distance):
    size = lax.axis_size("cam")
    return lax.ppermute(values, "cam", [(i, (i + distance) % size) for i in range(size)])


def ring_gather(values, half):
    before = shift_by(values, 1)
    after = shift_by(values, 3)
    return values, before, after, shift_by(before[:half], 1), shift_by(after[half:], 3)


def ring_halves(values, half):
    before_low = shift_by(values[:half], 1)
    after_high = shift_by(values[half:], 3)
    before_high = shift_by(values[half:], 1)
    after_low = shift_by(values[:half], 3)
    far = (shift_by(before_low, 1), shift_by(after_high, 3))
    return (values, before_low, before_high, after_low, after_high), far


def call(kernel, inputs, outputs, scratch=(), name=None):
    spaces = {"s": SMEM, "v": VMEM, "h": HBM}
    where = [spaces[kind] for kind, unused in inputs]
    several = isinstance(outputs, tuple)
    return pl.pallas_call(
        kernel,
        out_shape=outputs,
        in_specs=where,
        out_specs=tuple(VMEM for unused in outputs) if several else VMEM,
        scratch_shapes=list(scratch),
        compiler_params=PARAMS,
        name=name,
    )(*[value for unused, value in inputs])


def body(
    params,
    moment_first,
    moment_second,
    cam_proj,
    send_block,
    tile_slot,
    tile_count,
    targets,
    split_block,
    split_live,
):
    owned = params.shape[0]
    owners = split_block.shape[1]
    groups = lax.axis_size("cam")
    share = owned // groups
    place = lax.axis_index("cam").astype(jnp.int32).reshape(1)
    by_field = params.transpose(1, 0, 2)
    proj = cam_proj.transpose(1, 0, 2)
    send = send_block.reshape(2, owners)
    wire = shape(owners, PROJ, 2, LANES)
    rows = shape(2 * PROJ, owned, LANES)
    plane = pltpu.VMEM((2 * PROJ, owned, LANES), jnp.float32)

    def s(value):
        return ("s", value)

    def v(value):
        return ("v", value)

    outgoing, raw = pl.pallas_call(
        project_kernel,
        out_shape=(wire, rows),
        in_specs=[HBM, HBM, HBM],
        out_specs=(VMEM, VMEM),
        scratch_shapes=[
            pltpu.VMEM((FIELDS, owned, LANES), jnp.float32),
            pltpu.VMEM((2 * PROJ, owned, LANES), jnp.float32),
            pltpu.SMEM((PROJ, 2, FIELDS), jnp.float32),
            pltpu.SMEM((2, owners), jnp.int32),
            pltpu.SemaphoreType.DMA((6,)),
        ],
        compiler_params=PARAMS,
        name="project",
    )(proj, send, by_field)
    received = lax.all_to_all(outgoing, "dev", split_axis=0, concat_axis=0, tiled=True)

    projs = jnp.concatenate([proj, shift_by(proj, 1), shift_by(proj, 3), shift_by(proj, 2)], axis=1)
    plan = jnp.concatenate([tile_slot.reshape(2, 2 * KMAX), tile_count], axis=1)
    target = jnp.broadcast_to(targets.reshape(12, PIX, 1), (12, PIX, LANES))
    received, target, plan, projs = lax.optimization_barrier((received, target, plan, projs))

    returning, pictures = call(
        render_kernel, [s(plan), v(received), v(target)], (wire, shape(PIX, LANES)), RENDER_SCRATCH, "render"
    )
    returned = lax.all_to_all(returning, "dev", split_axis=0, concat_axis=0, tiled=True)

    first = moment_first.reshape(share, FIELDS, LANES).transpose(1, 0, 2)
    second = moment_second.reshape(share, FIELDS, LANES).transpose(1, 0, 2)
    first, second, returning = lax.optimization_barrier((first, second, returning))
    packed = call(
        pack_kernel, [s(place), v(first), v(second)], tuple(shape(2, QUARTER, share, LANES) for unused in range(4)), (), "pack"
    )
    moments = [packed[0]] + [shift_by(packed[ahead], ahead) for ahead in range(1, 4)]
    images = pictures[:, :12].T.reshape(targets.shape)
    returned, moments, images = lax.optimization_barrier((returned, moments, images))
    pulls = call(collect_kernel, [s(send), v(returned), v(raw)], rows, [plane], "collect")
    near, far = ring_halves(pulls, PROJ)
    near, far = [v(value) for value in near], [v(value) for value in far]
    grads = call(near_kernel, [s(place), s(projs)] + near, shape(QUARTER, owned, LANES), (), "near")
    fresh, parents = call(
        quarter_kernel,
        [s(place), s(split_block), s(split_live), s(projs), v(grads)]
        + far
        + [("h", by_field)]
        + [v(value) for value in moments],
        (shape(QUARTER, owned, LANES), shape(owners, PIECE, LANES)),
        [
            pltpu.VMEM((QUARTER, owned, LANES), jnp.float32),
            pltpu.VMEM((QUARTER, owned, LANES), jnp.float32),
            pltpu.SemaphoreType.DMA(()),
        ],
        "quarter",
    )
    parents = lax.all_to_all(parents, "dev", split_axis=0, concat_axis=0, tiled=True)
    own = shape(FIELDS, share, LANES)
    new_first, new_second = call(
        moments_kernel, [s(place), s(projs)] + near + far + [v(first), v(second)], (own, own), (), "moments"
    )
    fresh = [v(value) for value in ring_gather(fresh, QUARTER // 2)]
    new_params = call(assemble_kernel, [s(place)] + fresh, shape(FIELDS, owned, LANES), (), "assemble")
    parents, new_params, new_first, new_second = lax.optimization_barrier((parents, new_params, new_first, new_second))
    near, far = ring_halves(parents, owners // 2)
    batch = owners // 2
    steps = owners // batch

    half = steps // 2

    def lower(i, *unused):
        return (jnp.minimum(i, half - 1), 0, 0)

    def upper(i, *unused):
        return (jnp.maximum(i - half, 0), 0, 0)

    def block(index):
        return pl.BlockSpec((batch, PIECE, LANES), index)

    def ahead_of(piece):
        return jnp.where(piece == 0, 0, jnp.where(piece == 1, 3, 1))

    children = shape(owners, FIELDS, 2, LANES)
    part = (batch, QUARTER, 2, LANES)
    near_children = pl.pallas_call(
        near_children_kernel,
        out_shape=children,
        grid_spec=pltpu.PrefetchScalarGridSpec(
            num_scalar_prefetch=1,
            grid=(steps, 3),
            in_specs=[block(lambda i, *unused: (i, 0, 0)), block(lower), block(upper), block(lower), block(upper)],
            out_specs=pl.BlockSpec(part, lambda i, piece, at: (i, lax.rem(at[0] + ahead_of(piece), 4), 0, 0)),
        ),
        compiler_params=PARAMS,
        name="near_children",
    )(place, *near)
    children = pl.pallas_call(
        far_children_kernel,
        out_shape=children,
        grid_spec=pltpu.PrefetchScalarGridSpec(
            num_scalar_prefetch=1,
            grid=(steps,),
            in_specs=[block(lower), block(upper), pl.BlockSpec(memory_space=pl.ANY)],
            out_specs=pl.BlockSpec(part, lambda i, at: (i, lax.rem(at[0] + 2, 4), 0, 0)),
        ),
        input_output_aliases={3: 0},
        compiler_params=PARAMS,
        name="far_children",
    )(place, *far, near_children)

    def back(values):
        return values.transpose(1, 0, 2).reshape(moment_first.shape)

    return (
        images,
        new_params.transpose(1, 0, 2),
        back(new_first),
        back(new_second),
        children.transpose(0, 2, 1, 3),
    )


def solution(mesh):
    placed = (
        P("dev", None, None),
        P("dev", "cam", None, None, None),
        P("dev", "cam", None, None, None),
        P("cam", None, None),
        P("cam", "dev", None, None),
        P("cam", "dev", None),
        P("cam", "dev"),
        P("cam", "dev", None, None),
        P("dev", None),
        P("dev", None),
    )
    return jax.shard_map(
        body,
        mesh=mesh,
        in_specs=placed,
        out_specs=(
            P("cam", "dev", None, None),
            P("dev", None, None),
            P("dev", "cam", None, None, None),
            P("dev", "cam", None, None, None),
            P("dev", None, None, None),
        ),
        check_vma=False,
    )
```

```python
import math

import jax
import jax.numpy as jnp
from jax import lax
from jax.experimental import pallas as pl
from jax.experimental.pallas import tpu as pltpu
from jax.sharding import PartitionSpec as P

TSIDE = 16
PIX = TSIDE * TSIDE
LANES = 128
PROJ = 9
KMAX = 8
FIELDS = 59
QUARTER = 15
WIDTH = 5

LOSS_WEIGHT = 256.0
RATE = 0.01
BETA_FIRST = 0.9
BETA_SECOND = 0.999
EPSILON = 1e-08
SHRINK = math.log(1.6)
LOG2E = math.log2(math.e)

VMEM = pl.BlockSpec(memory_space=pltpu.VMEM)
SMEM = pl.BlockSpec(memory_space=pltpu.SMEM)
HBM = pl.BlockSpec(memory_space=pltpu.HBM)
PARAMS = pltpu.CompilerParams(vmem_limit_bytes=40 * 1024 * 1024)


def softplus(values):
    return jnp.maximum(values, 0.0) + jnp.log1p(jnp.exp(-jnp.abs(values)))


def sigmoid(values):
    return 1.0 / (1.0 + jnp.exp(-values))


def project_kernel(proj_in, send_in, params_ref, out_ref, raw_ref, held_ref, feat_ref, proj_ref, send_ref, sems):
    centre, spread = 0.5 * TSIDE, 0.375 * TSIDE
    copies = []
    for part, low in enumerate(range(0, FIELDS, QUARTER)):
        rows = pl.ds(low, min(QUARTER, FIELDS - low))
        copies.append(pltpu.make_async_copy(params_ref.at[rows], held_ref.at[rows], sems.at[part]))
        copies[-1].start()
    lists = pltpu.make_async_copy(send_in, send_ref, sems.at[4])
    weights = pltpu.make_async_copy(proj_in, proj_ref, sems.at[5])
    weights.start()
    lists.start()
    weights.wait()
    lists.wait()
    for part, copy in enumerate(copies):
        copy.wait()
        low = part * QUARTER
        for camera in range(2):
            raw = [None] * PROJ if part == 0 else [raw_ref[camera * PROJ + p] for p in range(PROJ)]
            for field in range(low, min(low + QUARTER, FIELDS)):
                row = held_ref[field]
                for p in range(PROJ):
                    term = proj_ref[p, camera, field] * row
                    raw[p] = term if field == 0 else raw[p] + term
            for p in range(PROJ):
                raw_ref[camera * PROJ + p] = raw[p]
    for camera in range(2):
        first = camera * PROJ
        raw = [raw_ref[first + p] for p in range(PROJ)]
        conic_a = 0.02 + 0.1 * softplus(raw[2])
        conic_c = 0.02 + 0.1 * softplus(raw[4])
        feat_ref[first + 0] = centre + spread * jnp.tanh(raw[0])
        feat_ref[first + 1] = centre + spread * jnp.tanh(raw[1])
        feat_ref[first + 2] = conic_a
        feat_ref[first + 3] = 0.9 * jnp.sqrt(conic_a * conic_c) * jnp.tanh(raw[3])
        feat_ref[first + 4] = conic_c
        feat_ref[first + 5] = 0.99 * sigmoid(raw[5] - 6.0)
        for p in range(6, PROJ):
            feat_ref[first + p] = sigmoid(raw[p])

    def place(j, unused):
        for camera in range(2):
            block = send_ref[camera, j]
            for p in range(PROJ):
                out_ref[j, p, pl.ds(camera, 1), :] = feat_ref[camera * PROJ + p, pl.ds(block, 1), :]
        return unused

    lax.fori_loop(0, out_ref.shape[0], place, 0, unroll=4)


SPLITS = 2


def split_parts(values):
    parts = []
    for at in range(SPLITS):
        part = values.astype(jnp.bfloat16)
        parts.append(part)
        if at < SPLITS - 1:
            values = values - part.astype(jnp.float32)
    return parts


def render_kernel(
    plan_ref,
    recv_ref,
    target_ref,
    back_ref,
    image_ref,
    alpha_ref,
    weight_ref,
    shade_ref,
    part_ref,
    before_ref,
    behind_ref,
    acc_ref,
    carry_ref,
):
    lane = lax.broadcasted_iota(jnp.int32, (PIX, LANES), 1)
    column = lax.broadcasted_iota(jnp.int32, (TSIDE, LANES), 0).astype(jnp.float32) + 0.5
    row = lax.broadcasted_iota(jnp.int32, (LANES, 2 * LANES), 0)
    col = lax.broadcasted_iota(jnp.int32, (LANES, 2 * LANES), 1)
    earlier = jnp.where((row < col) | (col >= LANES), 1.0, 0.0).astype(jnp.bfloat16)
    later = jnp.where((row > col) | (col >= LANES), 1.0, 0.0).astype(jnp.bfloat16)
    for at in range(SPLITS):
        before_ref[at * LANES : (at + 1) * LANES] = earlier
        behind_ref[at * LANES : (at + 1) * LANES] = later
    back_ref[...] = jnp.zeros(back_ref.shape, jnp.float32)
    image_ref[...] = jnp.zeros(image_ref.shape, jnp.float32)

    def tile(index, unused):
        camera = index // 2
        which = index % 2
        count = plan_ref[camera, 2 * KMAX + which]
        pairs = (count + 1) // 2

        def slot_at(k):
            return plan_ref[camera, which * KMAX + jnp.minimum(k, count - 1)]

        def feature(slot, p):
            return recv_ref[slot, p, pl.ds(camera, 1), :]

        def put_parts(start, values):
            for at, part in enumerate(split_parts(values)):
                part_ref[start : start + values.shape[0], at * LANES : (at + 1) * LANES] = part

        carry_ref[...] = jnp.zeros(carry_ref.shape, jnp.float32)
        acc_ref[...] = jnp.zeros(acc_ref.shape, jnp.float32)

        def forward(pair, unused):
            slots = [slot_at(pair * 2 + e) for e in range(2)]
            for e in range(2):
                k = pair * 2 + e
                slot = slots[e]
                opacity = jnp.where(k < count, feature(slot, 5), 0.0)
                off_x = column - feature(slot, 0)
                mean_y = feature(slot, 1)
                half_a = (-0.5 * LOG2E) * feature(slot, 2)
                full_b = -LOG2E * feature(slot, 3)
                half_c = (-0.5 * LOG2E) * feature(slot, 4)
                square_x = half_a * off_x * off_x
                for y in range(TSIDE):
                    off_y = (y + 0.5) - mean_y
                    alpha = opacity * jnp.exp2(square_x + ((full_b * off_y) * off_x + half_c * off_y * off_y))
                    alpha_ref[k, y * TSIDE : (y + 1) * TSIDE] = alpha
                    put_parts(e * PIX + y * TSIDE, jnp.log(1.0 - alpha))
            sums = jnp.dot(part_ref[...], before_ref[...], preferred_element_type=jnp.float32)
            colours = [[feature(slots[e], 6 + c) for c in range(3)] for e in range(2)]
            for y in range(TSIDE):
                rows = slice(y * TSIDE, (y + 1) * TSIDE)
                next_rows = slice(PIX + y * TSIDE, PIX + (y + 1) * TSIDE)
                carry = carry_ref[rows]
                weights = [alpha_ref[pair * 2, rows] * jnp.exp(carry + sums[rows, :LANES])]
                carry = carry + sums[rows, LANES:]
                weights.append(alpha_ref[pair * 2 + 1, rows] * jnp.exp(carry + sums[next_rows, :LANES]))
                carry_ref[rows] = carry + sums[next_rows, LANES:]
                weight_ref[pair * 2, rows] = weights[0]
                weight_ref[pair * 2 + 1, rows] = weights[1]
                for c in range(3):
                    acc_ref[c, rows] = acc_ref[c, rows] + (colours[0][c] * weights[0] + colours[1][c] * weights[1])
            return unused

        lax.fori_loop(0, pairs, forward, 0)
        for c in range(3):
            place = index * 3 + c
            put_parts(0, acc_ref[c])
            colour = jnp.dot(part_ref[:PIX], before_ref[:, LANES:], preferred_element_type=jnp.float32)
            image_ref[...] = jnp.where(lane == place, colour, image_ref[...])
            acc_ref[c] = LOSS_WEIGHT * (colour - target_ref[place])
        carry_ref[...] = jnp.zeros(carry_ref.shape, jnp.float32)

        def backward(step, unused):
            pair = pairs - 1 - step
            slots = [slot_at(pair * 2 + e) for e in range(2)]
            colour_grads = []
            for e in range(2):
                k = pair * 2 + e
                colours = [feature(slots[e], 6 + c) for c in range(3)]
                sums_c = [None] * 3
                for y in range(TSIDE):
                    rows = slice(y * TSIDE, (y + 1) * TSIDE)
                    weights = weight_ref[k, rows]
                    cots = [acc_ref[c, rows] for c in range(3)]
                    shade = (colours[0] * cots[0] + colours[1] * cots[1] + colours[2] * cots[2]) * weights
                    shade_ref[e, rows] = shade
                    put_parts(e * PIX + y * TSIDE, shade)
                    for c in range(3):
                        term = cots[c] * weights
                        sums_c[c] = term if y == 0 else sums_c[c] + term
                colour_grads.append(sums_c)
            sums = jnp.dot(part_ref[...], behind_ref[...], preferred_element_type=jnp.float32)
            for e in (1, 0):
                k = pair * 2 + e
                slot = slots[e]
                off_x = column - feature(slot, 0)
                mean_y = feature(slot, 1)
                plain, first_y, second_y = None, None, None
                for y in range(TSIDE):
                    rows = slice(y * TSIDE, (y + 1) * TSIDE)
                    inside = slice(e * PIX + y * TSIDE, e * PIX + (y + 1) * TSIDE)
                    carry = carry_ref[rows]
                    alpha = alpha_ref[k, rows]
                    keep = 1.0 - alpha
                    inverse = pl.reciprocal(keep, approx=True)
                    inverse = inverse * (2.0 - keep * inverse)
                    pull = shade_ref[e, rows] - (carry + sums[inside, :LANES]) * (alpha * inverse)
                    carry_ref[rows] = carry + sums[inside, LANES:]
                    off_y = (y + 0.5) - mean_y
                    once = off_y * pull
                    twice = off_y * once
                    plain = pull if y == 0 else plain + pull
                    first_y = once if y == 0 else first_y + once
                    second_y = twice if y == 0 else second_y + twice

                def total(values):
                    return jnp.sum(values, axis=0, keepdims=True)

                along_x = off_x * plain
                sum_x = total(along_x)
                sum_y = total(first_y)
                conic_a, conic_b, conic_c = feature(slot, 2), feature(slot, 3), feature(slot, 4)
                grads = [
                    conic_a * sum_x + conic_b * sum_y,
                    conic_b * sum_x + conic_c * sum_y,
                    -0.5 * total(off_x * along_x),
                    -total(off_x * first_y),
                    -0.5 * total(second_y),
                    total(plain),
                ] + [total(values) for values in colour_grads[e]]
                for p in range(PROJ):
                    spot = (slot, p, pl.ds(camera, 1), slice(None))
                    back_ref[spot] = back_ref[spot] + grads[p]
            return unused

        lax.fori_loop(0, pairs, backward, 0)
        return unused

    lax.fori_loop(0, 4, tile, 0)


RENDER_SCRATCH = [
    pltpu.VMEM((8, PIX, LANES), jnp.float32),
    pltpu.VMEM((8, PIX, LANES), jnp.float32),
    pltpu.VMEM((2, PIX, LANES), jnp.float32),
    pltpu.VMEM((2 * PIX, SPLITS * LANES), jnp.bfloat16),
    pltpu.VMEM((SPLITS * LANES, 2 * LANES), jnp.bfloat16),
    pltpu.VMEM((SPLITS * LANES, 2 * LANES), jnp.bfloat16),
    pltpu.VMEM((3, PIX, LANES), jnp.float32),
    pltpu.VMEM((PIX, LANES), jnp.float32),
]


def collect_kernel(send_ref, back_ref, raw_ref, out_ref, acc_ref):
    acc_ref[...] = jnp.zeros(acc_ref.shape, jnp.float32)

    def gather(j, unused):
        for camera in range(2):
            block = send_ref[camera, j]
            for p in range(PROJ):
                spot = (camera * PROJ + p, pl.ds(block, 1), slice(None))
                acc_ref[spot] = acc_ref[spot] + back_ref[j, p, pl.ds(camera, 1), :]
        return unused

    lax.fori_loop(0, back_ref.shape[0], gather, 0, unroll=4)
    spread = 0.375 * TSIDE
    for camera in range(2):
        first = camera * PROJ
        raw = [raw_ref[first + p] for p in range(PROJ)]
        grad = [acc_ref[first + p] for p in range(PROJ)]
        conic_a = 0.02 + 0.1 * softplus(raw[2])
        conic_c = 0.02 + 0.1 * softplus(raw[4])
        root = 0.9 * jnp.sqrt(conic_a * conic_c)
        turn = jnp.tanh(raw[3])
        from_b = 0.5 * grad[3] * root * turn
        tan_x, tan_y = jnp.tanh(raw[0]), jnp.tanh(raw[1])
        result = [
            grad[0] * spread * (1.0 - tan_x * tan_x),
            grad[1] * spread * (1.0 - tan_y * tan_y),
            (grad[2] + from_b / conic_a) * 0.1 * sigmoid(raw[2]),
            grad[3] * root * (1.0 - turn * turn),
            (grad[4] + from_b / conic_c) * 0.1 * sigmoid(raw[4]),
            grad[5] * (1.0 - sigmoid(raw[5] - 6.0)),
        ]
        for p in range(6, PROJ):
            shade = sigmoid(raw[p])
            result.append(grad[p] * shade * (1.0 - shade))
        for p in range(PROJ):
            out_ref[first + p] = result[p]


def pack_kernel(place_ref, first_ref, second_ref, *out_refs):
    for ahead, out_ref in enumerate(out_refs):
        quarter = lax.rem(place_ref[0] + ahead, 4)
        for field in range(QUARTER):
            at = jnp.minimum(quarter * QUARTER + field, FIELDS - 1)
            out_ref[0, field] = first_ref[at]
            out_ref[1, field] = second_ref[at]


def step_of(first, second, old, grad):
    new_first = BETA_FIRST * first + (1.0 - BETA_FIRST) * grad
    new_second = BETA_SECOND * second + (1.0 - BETA_SECOND) * grad * grad
    return new_first, new_second, old - RATE * new_first / (jnp.sqrt(new_second) + EPSILON)


def add_up(grads, proj_ref, source, low_ref, high_ref, blocks, fields):
    for row in range(2 * PROJ):
        value = low_ref[row, blocks, :] if row < PROJ else high_ref[row - PROJ, blocks, :]
        for at, field in enumerate(fields):
            term = proj_ref[row % PROJ, 2 * source + row // PROJ, field] * value
            grads[at] = term if grads[at] is None else grads[at] + term


def quarter_fields(place_ref, low):
    return [jnp.minimum(place_ref[0] * QUARTER + low + at, FIELDS - 1) for at in range(WIDTH)]


def near_kernel(place_ref, proj_ref, own_ref, before_low, before_high, after_low, after_high, grad_ref):
    for low in range(0, QUARTER, WIDTH):
        grads = [None] * WIDTH
        fields = quarter_fields(place_ref, low)
        own = (own_ref.at[pl.ds(0, PROJ)], own_ref.at[pl.ds(PROJ, PROJ)])
        for source, halves in enumerate((own, (before_low, before_high), (after_low, after_high))):
            add_up(grads, proj_ref, source, *halves, slice(None), fields)
        for at in range(WIDTH):
            grad_ref[low + at] = grads[at]


def quarter_kernel(
    place_ref,
    block_ref,
    live_ref,
    proj_ref,
    near_ref,
    far_low,
    far_high,
    params_ref,
    moment_0,
    moment_1,
    moment_2,
    moment_3,
    new_ref,
    parents_ref,
    grad_ref,
    held_ref,
    sem,
):
    share = moment_0.shape[2]
    base = place_ref[0] * QUARTER
    start = jnp.minimum(base, FIELDS - QUARTER)
    copy = pltpu.make_async_copy(params_ref.at[pl.ds(start, QUARTER)], held_ref, sem)
    copy.start()
    for low in range(0, QUARTER, WIDTH):
        grads = [near_ref[low + at] for at in range(WIDTH)]
        add_up(grads, proj_ref, 3, far_low, far_high, slice(None), quarter_fields(place_ref, low))
        for at in range(WIDTH):
            grad_ref[low + at] = grads[at]
    copy.wait()
    for ahead, moment_ref in enumerate((moment_0, moment_1, moment_2, moment_3)):
        blocks = pl.ds(pl.multiple_of(lax.rem(place_ref[0] + (4 - ahead), 4) * share, share), share)
        for field in range(QUARTER):
            old = held_ref[jnp.minimum(base - start + field, QUARTER - 1), blocks, :]
            new = step_of(moment_ref[0, field], moment_ref[1, field], old, grad_ref[field, blocks, :])[2]
            new_ref[field, blocks, :] = new

    def place(j, unused):
        block = block_ref[0, j]
        live = live_ref[0, j] == 1
        for field in range(QUARTER):
            parents_ref[j, field] = jnp.where(live, new_ref[field, pl.ds(block, 1), :], jnp.nan)
        return unused

    lax.fori_loop(0, parents_ref.shape[0], place, 0, unroll=8)


def moments_kernel(
    place_ref,
    proj_ref,
    own_ref,
    before_low,
    before_high,
    after_low,
    after_high,
    far_low,
    far_high,
    first_ref,
    second_ref,
    new_first_ref,
    new_second_ref,
):
    share = first_ref.shape[1]
    blocks = pl.ds(pl.multiple_of(place_ref[0] * share, share), share)
    own = (own_ref.at[pl.ds(0, PROJ)], own_ref.at[pl.ds(PROJ, PROJ)])
    sources = (own, (before_low, before_high), (after_low, after_high), (far_low, far_high))
    width = 12
    for low in range(0, FIELDS, width):
        fields = range(low, min(low + width, FIELDS))
        grads = [None] * len(fields)
        for source, halves in enumerate(sources):
            add_up(grads, proj_ref, source, *halves, blocks, fields)
        for at, field in enumerate(fields):
            first, second, unused = step_of(first_ref[field], second_ref[field], 0.0, grads[at])
            new_first_ref[field] = first
            new_second_ref[field] = second


def assemble_kernel(place_ref, own_ref, before_ref, after_ref, low_ref, high_ref, out_ref):
    for field in range(QUARTER - 1, -1, -1):
        half = low_ref.shape[0]
        far = low_ref[field] if field < half else high_ref[field - half]
        rows = ((0, own_ref[field]), (3, before_ref[field]), (1, after_ref[field]), (2, far))
        for ahead, value in rows:
            quarter = lax.rem(place_ref[0] + ahead, 4)
            out_ref[jnp.minimum(quarter * QUARTER + field, FIELDS - 1)] = value


def fill_children(ref, quarter, out_ref):
    first = quarter == 0

    def one(j, unused):
        sign = jnp.where(lax.broadcasted_iota(jnp.int32, (2, LANES), 0) == 0, 0.5, -0.5)
        rows = [jnp.broadcast_to(ref[j, field], (2, LANES)) for field in range(QUARTER)]
        for field in range(QUARTER):
            row = rows[field]
            if field < 3:
                row = row + jnp.where(first, sign * jnp.exp(rows[field + 3] - 1.0), 0.0)
            elif field < 6:
                row = row - jnp.where(first, SHRINK, 0.0)
            out_ref[j, field] = jnp.where(row != row, 0.0, row)
        return unused

    lax.fori_loop(0, out_ref.shape[0], one, 0, unroll=8)


def near_children_kernel(place_ref, own_ref, before_low, before_high, after_low, after_high, out_ref):
    upper = pl.program_id(0) >= pl.num_programs(0) // 2
    piece = pl.program_id(1)

    @pl.when(piece == 0)
    def _():
        fill_children(own_ref, place_ref[0], out_ref)

    for at, ahead, low, high in ((1, 3, before_low, before_high), (2, 1, after_low, after_high)):

        @pl.when((piece == at) & jnp.logical_not(upper))
        def _():
            fill_children(low, lax.rem(place_ref[0] + ahead, 4), out_ref)

        @pl.when((piece == at) & upper)
        def _():
            fill_children(high, lax.rem(place_ref[0] + ahead, 4), out_ref)


def far_children_kernel(place_ref, far_low, far_high, near_ref, out_ref):
    upper = pl.program_id(0) >= pl.num_programs(0) // 2
    quarter = lax.rem(place_ref[0] + 2, 4)

    @pl.when(jnp.logical_not(upper))
    def _():
        fill_children(far_low, quarter, out_ref)

    @pl.when(upper)
    def _():
        fill_children(far_high, quarter, out_ref)


def shape(*dims):
    return jax.ShapeDtypeStruct(dims, jnp.float32)


def shift_by(values, distance):
    size = lax.axis_size("cam")
    return lax.ppermute(values, "cam", [(i, (i + distance) % size) for i in range(size)])


def ring_gather(values, half):
    before = shift_by(values, 1)
    after = shift_by(values, 3)
    return values, before, after, shift_by(before[:half], 1), shift_by(after[half:], 3)


def ring_halves(values, half):
    before_low = shift_by(values[:half], 1)
    after_high = shift_by(values[half:], 3)
    before_high = shift_by(values[half:], 1)
    after_low = shift_by(values[:half], 3)
    far = (shift_by(before_low, 1), shift_by(after_high, 3))
    return (values, before_low, before_high, after_low, after_high), far


def call(kernel, inputs, outputs, scratch=(), name=None):
    spaces = {"s": SMEM, "v": VMEM, "h": HBM}
    where = [spaces[kind] for kind, unused in inputs]
    several = isinstance(outputs, tuple)
    return pl.pallas_call(
        kernel,
        out_shape=outputs,
        in_specs=where,
        out_specs=tuple(VMEM for unused in outputs) if several else VMEM,
        scratch_shapes=list(scratch),
        compiler_params=PARAMS,
        name=name,
    )(*[value for unused, value in inputs])


def body(
    params,
    moment_first,
    moment_second,
    cam_proj,
    send_block,
    tile_slot,
    tile_count,
    targets,
    split_block,
    split_live,
):
    owned = params.shape[0]
    owners = split_block.shape[1]
    groups = lax.axis_size("cam")
    share = owned // groups
    place = lax.axis_index("cam").astype(jnp.int32).reshape(1)
    by_field = params.transpose(1, 0, 2)
    proj = cam_proj.transpose(1, 0, 2)
    send = send_block.reshape(2, owners)
    wire = shape(owners, PROJ, 2, LANES)
    rows = shape(2 * PROJ, owned, LANES)
    plane = pltpu.VMEM((2 * PROJ, owned, LANES), jnp.float32)

    def s(value):
        return ("s", value)

    def v(value):
        return ("v", value)

    outgoing, raw = pl.pallas_call(
        project_kernel,
        out_shape=(wire, rows),
        in_specs=[HBM, HBM, HBM],
        out_specs=(VMEM, VMEM),
        scratch_shapes=[
            pltpu.VMEM((FIELDS, owned, LANES), jnp.float32),
            pltpu.VMEM((2 * PROJ, owned, LANES), jnp.float32),
            pltpu.SMEM((PROJ, 2, FIELDS), jnp.float32),
            pltpu.SMEM((2, owners), jnp.int32),
            pltpu.SemaphoreType.DMA((6,)),
        ],
        compiler_params=pltpu.CompilerParams(vmem_limit_bytes=62 * 1024 * 1024),
        name="project",
    )(proj, send, by_field)
    received = lax.all_to_all(outgoing, "dev", split_axis=0, concat_axis=0, tiled=True)

    projs = jnp.concatenate([proj, shift_by(proj, 1), shift_by(proj, 3), shift_by(proj, 2)], axis=1)
    plan = jnp.concatenate([tile_slot.reshape(2, 2 * KMAX), tile_count], axis=1)
    target = jnp.broadcast_to(targets.reshape(12, PIX, 1), (12, PIX, LANES))
    received, target, plan, projs = lax.optimization_barrier((received, target, plan, projs))

    returning, pictures = call(
        render_kernel, [s(plan), v(received), v(target)], (wire, shape(PIX, LANES)), RENDER_SCRATCH, "render"
    )
    returned = lax.all_to_all(returning, "dev", split_axis=0, concat_axis=0, tiled=True)

    first = moment_first.reshape(share, FIELDS, LANES).transpose(1, 0, 2)
    second = moment_second.reshape(share, FIELDS, LANES).transpose(1, 0, 2)
    first, second, returning = lax.optimization_barrier((first, second, returning))
    packed = call(
        pack_kernel, [s(place), v(first), v(second)], tuple(shape(2, QUARTER, share, LANES) for unused in range(4)), (), "pack"
    )
    moments = [packed[0]] + [shift_by(packed[ahead], ahead) for ahead in range(1, 4)]
    images = pictures[:, :12].T.reshape(targets.shape)
    returned, moments, images = lax.optimization_barrier((returned, moments, images))
    pulls = call(collect_kernel, [s(send), v(returned), v(raw)], rows, [plane], "collect")
    near, far = ring_halves(pulls, PROJ)
    near, far = [v(value) for value in near], [v(value) for value in far]
    grads = call(near_kernel, [s(place), s(projs)] + near, shape(QUARTER, owned, LANES), (), "near")
    fresh, parents = call(
        quarter_kernel,
        [s(place), s(split_block), s(split_live), s(projs), v(grads)]
        + far
        + [("h", by_field)]
        + [v(value) for value in moments],
        (shape(QUARTER, owned, LANES), shape(owners, QUARTER, 1, LANES)),
        [
            pltpu.VMEM((QUARTER, owned, LANES), jnp.float32),
            pltpu.VMEM((QUARTER, owned, LANES), jnp.float32),
            pltpu.SemaphoreType.DMA(()),
        ],
        "quarter",
    )
    parents = lax.all_to_all(parents, "dev", split_axis=0, concat_axis=0, tiled=True)
    own = shape(FIELDS, share, LANES)
    new_first, new_second = call(
        moments_kernel, [s(place), s(projs)] + near + far + [v(first), v(second)], (own, own), (), "moments"
    )
    fresh = [v(value) for value in ring_gather(fresh, QUARTER // 2)]
    new_params = call(assemble_kernel, [s(place)] + fresh, shape(FIELDS, owned, LANES), (), "assemble")
    parents, new_params, new_first, new_second = lax.optimization_barrier((parents, new_params, new_first, new_second))
    near, far = ring_halves(parents, owners // 2)
    batch = owners // 2
    steps = owners // batch

    half = steps // 2

    def lower(i, *unused):
        return (jnp.minimum(i, half - 1), 0, 0, 0)

    def upper(i, *unused):
        return (jnp.maximum(i - half, 0), 0, 0, 0)

    def block(index):
        return pl.BlockSpec((batch, QUARTER, 1, LANES), index)

    def ahead_of(piece):
        return jnp.where(piece == 0, 0, jnp.where(piece == 1, 3, 1))

    children = shape(owners, FIELDS, 2, LANES)
    part = (batch, QUARTER, 2, LANES)
    near_children = pl.pallas_call(
        near_children_kernel,
        out_shape=children,
        grid_spec=pltpu.PrefetchScalarGridSpec(
            num_scalar_prefetch=1,
            grid=(steps, 3),
            in_specs=[block(lambda i, *unused: (i, 0, 0, 0)), block(lower), block(upper), block(lower), block(upper)],
            out_specs=pl.BlockSpec(part, lambda i, piece, at: (i, lax.rem(at[0] + ahead_of(piece), 4), 0, 0)),
        ),
        compiler_params=PARAMS,
        name="near_children",
    )(place, *near)
    children = pl.pallas_call(
        far_children_kernel,
        out_shape=children,
        grid_spec=pltpu.PrefetchScalarGridSpec(
            num_scalar_prefetch=1,
            grid=(steps,),
            in_specs=[block(lower), block(upper), pl.BlockSpec(memory_space=pl.ANY)],
            out_specs=pl.BlockSpec(part, lambda i, at: (i, lax.rem(at[0] + 2, 4), 0, 0)),
        ),
        input_output_aliases={3: 0},
        compiler_params=PARAMS,
        name="far_children",
    )(place, *far, near_children)

    def back(values):
        return values.transpose(1, 0, 2).reshape(moment_first.shape)

    return (
        images,
        new_params.transpose(1, 0, 2),
        back(new_first),
        back(new_second),
        children.transpose(0, 2, 1, 3),
    )


def solution(mesh):
    placed = (
        P("dev", None, None),
        P("dev", "cam", None, None, None),
        P("dev", "cam", None, None, None),
        P("cam", None, None),
        P("cam", "dev", None, None),
        P("cam", "dev", None),
        P("cam", "dev"),
        P("cam", "dev", None, None),
        P("dev", None),
        P("dev", None),
    )
    return jax.shard_map(
        body,
        mesh=mesh,
        in_specs=placed,
        out_specs=(
            P("cam", "dev", None, None),
            P("dev", None, None),
            P("dev", "cam", None, None, None),
            P("dev", "cam", None, None, None),
            P("dev", None, None, None),
        ),
        check_vma=False,
    )
```

```python
import math

import jax
import jax.numpy as jnp
from jax import lax
from jax.experimental import pallas as pl
from jax.experimental.pallas import tpu as pltpu
from jax.sharding import PartitionSpec as P

TSIDE = 16
PIX = TSIDE * TSIDE
LANES = 128
PROJ = 9
KMAX = 8
FIELDS = 59
QUARTER = 15
WIDTH = 5

LOSS_WEIGHT = 256.0
RATE = 0.01
BETA_FIRST = 0.9
BETA_SECOND = 0.999
EPSILON = 1e-08
SHRINK = math.log(1.6)
LOG2E = math.log2(math.e)

VMEM = pl.BlockSpec(memory_space=pltpu.VMEM)
SMEM = pl.BlockSpec(memory_space=pltpu.SMEM)
HBM = pl.BlockSpec(memory_space=pltpu.HBM)
PARAMS = pltpu.CompilerParams(vmem_limit_bytes=40 * 1024 * 1024)


def softplus(values):
    return jnp.maximum(values, 0.0) + jnp.log1p(jnp.exp(-jnp.abs(values)))


def sigmoid(values):
    return 1.0 / (1.0 + jnp.exp(-values))


def project_kernel(proj_in, send_in, params_ref, out_ref, raw_ref, held_ref, feat_ref, proj_ref, send_ref, sems):
    centre, spread = 0.5 * TSIDE, 0.375 * TSIDE
    copies = []
    for part, low in enumerate(range(0, FIELDS, QUARTER)):
        rows = pl.ds(low, min(QUARTER, FIELDS - low))
        copies.append(pltpu.make_async_copy(params_ref.at[rows], held_ref.at[rows], sems.at[part]))
        copies[-1].start()
    lists = pltpu.make_async_copy(send_in, send_ref, sems.at[4])
    weights = pltpu.make_async_copy(proj_in, proj_ref, sems.at[5])
    weights.start()
    lists.start()
    weights.wait()
    lists.wait()
    for part, copy in enumerate(copies):
        copy.wait()
        low = part * QUARTER
        for camera in range(2):
            raw = [None] * PROJ if part == 0 else [raw_ref[camera * PROJ + p] for p in range(PROJ)]
            for field in range(low, min(low + QUARTER, FIELDS)):
                row = held_ref[field]
                for p in range(PROJ):
                    term = proj_ref[p, camera, field] * row
                    raw[p] = term if field == 0 else raw[p] + term
            for p in range(PROJ):
                raw_ref[camera * PROJ + p] = raw[p]
    for camera in range(2):
        first = camera * PROJ
        raw = [raw_ref[first + p] for p in range(PROJ)]
        conic_a = 0.02 + 0.1 * softplus(raw[2])
        conic_c = 0.02 + 0.1 * softplus(raw[4])
        feat_ref[first + 0] = centre + spread * jnp.tanh(raw[0])
        feat_ref[first + 1] = centre + spread * jnp.tanh(raw[1])
        feat_ref[first + 2] = conic_a
        feat_ref[first + 3] = 0.9 * jnp.sqrt(conic_a * conic_c) * jnp.tanh(raw[3])
        feat_ref[first + 4] = conic_c
        feat_ref[first + 5] = 0.99 * sigmoid(raw[5] - 6.0)
        for p in range(6, PROJ):
            feat_ref[first + p] = sigmoid(raw[p])

    def place(j, unused):
        for camera in range(2):
            block = send_ref[camera, j]
            for p in range(PROJ):
                out_ref[j, p, pl.ds(camera, 1), :] = feat_ref[camera * PROJ + p, pl.ds(block, 1), :]
        return unused

    lax.fori_loop(0, out_ref.shape[0], place, 0, unroll=4)


SPLITS = 2


def split_parts(values):
    parts = []
    for at in range(SPLITS):
        part = values.astype(jnp.bfloat16)
        parts.append(part)
        if at < SPLITS - 1:
            values = values - part.astype(jnp.float32)
    return parts


def render_kernel(
    plan_ref,
    recv_ref,
    target_ref,
    back_ref,
    image_ref,
    alpha_ref,
    weight_ref,
    shade_ref,
    part_ref,
    before_ref,
    behind_ref,
    acc_ref,
    carry_ref,
):
    lane = lax.broadcasted_iota(jnp.int32, (PIX, LANES), 1)
    column = lax.broadcasted_iota(jnp.int32, (TSIDE, LANES), 0).astype(jnp.float32) + 0.5
    row = lax.broadcasted_iota(jnp.int32, (LANES, 2 * LANES), 0)
    col = lax.broadcasted_iota(jnp.int32, (LANES, 2 * LANES), 1)
    earlier = jnp.where((row < col) | (col >= LANES), 1.0, 0.0).astype(jnp.bfloat16)
    later = jnp.where((row > col) | (col >= LANES), 1.0, 0.0).astype(jnp.bfloat16)
    for at in range(SPLITS):
        before_ref[at * LANES : (at + 1) * LANES] = earlier
        behind_ref[at * LANES : (at + 1) * LANES] = later
    back_ref[...] = jnp.zeros(back_ref.shape, jnp.float32)
    image_ref[...] = jnp.zeros(image_ref.shape, jnp.float32)

    def tile(index, unused):
        camera = index // 2
        which = index % 2
        count = plan_ref[camera, 2 * KMAX + which]
        pairs = (count + 1) // 2

        def slot_at(k):
            return plan_ref[camera, which * KMAX + jnp.minimum(k, count - 1)]

        def feature(slot, p):
            return recv_ref[slot, p, pl.ds(camera, 1), :]

        def put_parts(start, values):
            for at, part in enumerate(split_parts(values)):
                part_ref[start : start + values.shape[0], at * LANES : (at + 1) * LANES] = part

        carry_ref[...] = jnp.zeros(carry_ref.shape, jnp.float32)
        acc_ref[...] = jnp.zeros(acc_ref.shape, jnp.float32)

        def forward(pair, unused):
            slots = [slot_at(pair * 2 + e) for e in range(2)]
            for e in range(2):
                k = pair * 2 + e
                slot = slots[e]
                opacity = jnp.where(k < count, feature(slot, 5), 0.0)
                off_x = column - feature(slot, 0)
                mean_y = feature(slot, 1)
                half_a = (-0.5 * LOG2E) * feature(slot, 2)
                full_b = -LOG2E * feature(slot, 3)
                half_c = (-0.5 * LOG2E) * feature(slot, 4)
                square_x = half_a * off_x * off_x
                for y in range(TSIDE):
                    off_y = (y + 0.5) - mean_y
                    alpha = opacity * jnp.exp2(square_x + ((full_b * off_y) * off_x + half_c * off_y * off_y))
                    alpha_ref[k, y * TSIDE : (y + 1) * TSIDE] = alpha
                    put_parts(e * PIX + y * TSIDE, jnp.log(1.0 - alpha))
            sums = jnp.dot(part_ref[...], before_ref[...], preferred_element_type=jnp.float32)
            colours = [[feature(slots[e], 6 + c) for c in range(3)] for e in range(2)]
            for y in range(TSIDE):
                rows = slice(y * TSIDE, (y + 1) * TSIDE)
                next_rows = slice(PIX + y * TSIDE, PIX + (y + 1) * TSIDE)
                carry = carry_ref[rows]
                weights = [alpha_ref[pair * 2, rows] * jnp.exp(carry + sums[rows, :LANES])]
                carry = carry + sums[rows, LANES:]
                weights.append(alpha_ref[pair * 2 + 1, rows] * jnp.exp(carry + sums[next_rows, :LANES]))
                carry_ref[rows] = carry + sums[next_rows, LANES:]
                weight_ref[pair * 2, rows] = weights[0]
                weight_ref[pair * 2 + 1, rows] = weights[1]
                for c in range(3):
                    acc_ref[c, rows] = acc_ref[c, rows] + (colours[0][c] * weights[0] + colours[1][c] * weights[1])
            return unused

        lax.fori_loop(0, pairs, forward, 0)
        for c in range(3):
            place = index * 3 + c
            put_parts(0, acc_ref[c])
            colour = jnp.dot(part_ref[:PIX], before_ref[:, LANES:], preferred_element_type=jnp.float32)
            image_ref[...] = jnp.where(lane == place, colour, image_ref[...])
            acc_ref[c] = LOSS_WEIGHT * (colour - target_ref[place])
        carry_ref[...] = jnp.zeros(carry_ref.shape, jnp.float32)

        def backward(step, unused):
            pair = pairs - 1 - step
            slots = [slot_at(pair * 2 + e) for e in range(2)]
            colour_grads = []
            for e in range(2):
                k = pair * 2 + e
                colours = [feature(slots[e], 6 + c) for c in range(3)]
                sums_c = [None] * 3
                for y in range(TSIDE):
                    rows = slice(y * TSIDE, (y + 1) * TSIDE)
                    weights = weight_ref[k, rows]
                    cots = [acc_ref[c, rows] for c in range(3)]
                    shade = (colours[0] * cots[0] + colours[1] * cots[1] + colours[2] * cots[2]) * weights
                    shade_ref[e, rows] = shade
                    put_parts(e * PIX + y * TSIDE, shade)
                    for c in range(3):
                        term = cots[c] * weights
                        sums_c[c] = term if y == 0 else sums_c[c] + term
                colour_grads.append(sums_c)
            sums = jnp.dot(part_ref[...], behind_ref[...], preferred_element_type=jnp.float32)
            for e in (1, 0):
                k = pair * 2 + e
                slot = slots[e]
                off_x = column - feature(slot, 0)
                mean_y = feature(slot, 1)
                plain, first_y, second_y = None, None, None
                for y in range(TSIDE):
                    rows = slice(y * TSIDE, (y + 1) * TSIDE)
                    inside = slice(e * PIX + y * TSIDE, e * PIX + (y + 1) * TSIDE)
                    carry = carry_ref[rows]
                    alpha = alpha_ref[k, rows]
                    keep = 1.0 - alpha
                    inverse = pl.reciprocal(keep, approx=True)
                    inverse = inverse * (2.0 - keep * inverse)
                    pull = shade_ref[e, rows] - (carry + sums[inside, :LANES]) * (alpha * inverse)
                    carry_ref[rows] = carry + sums[inside, LANES:]
                    off_y = (y + 0.5) - mean_y
                    once = off_y * pull
                    twice = off_y * once
                    plain = pull if y == 0 else plain + pull
                    first_y = once if y == 0 else first_y + once
                    second_y = twice if y == 0 else second_y + twice

                def total(values):
                    return jnp.sum(values, axis=0, keepdims=True)

                along_x = off_x * plain
                sum_x = total(along_x)
                sum_y = total(first_y)
                conic_a, conic_b, conic_c = feature(slot, 2), feature(slot, 3), feature(slot, 4)
                grads = [
                    conic_a * sum_x + conic_b * sum_y,
                    conic_b * sum_x + conic_c * sum_y,
                    -0.5 * total(off_x * along_x),
                    -total(off_x * first_y),
                    -0.5 * total(second_y),
                    total(plain),
                ] + [total(values) for values in colour_grads[e]]
                for p in range(PROJ):
                    spot = (slot, p, pl.ds(camera, 1), slice(None))
                    back_ref[spot] = back_ref[spot] + grads[p]
            return unused

        lax.fori_loop(0, pairs, backward, 0)
        return unused

    lax.fori_loop(0, 4, tile, 0)


RENDER_SCRATCH = [
    pltpu.VMEM((8, PIX, LANES), jnp.float32),
    pltpu.VMEM((8, PIX, LANES), jnp.float32),
    pltpu.VMEM((2, PIX, LANES), jnp.float32),
    pltpu.VMEM((2 * PIX, SPLITS * LANES), jnp.bfloat16),
    pltpu.VMEM((SPLITS * LANES, 2 * LANES), jnp.bfloat16),
    pltpu.VMEM((SPLITS * LANES, 2 * LANES), jnp.bfloat16),
    pltpu.VMEM((3, PIX, LANES), jnp.float32),
    pltpu.VMEM((PIX, LANES), jnp.float32),
]


def collect_kernel(send_ref, back_ref, raw_ref, out_ref, acc_ref):
    acc_ref[...] = jnp.zeros(acc_ref.shape, jnp.float32)

    def gather(j, unused):
        for camera in range(2):
            block = send_ref[camera, j]
            for p in range(PROJ):
                spot = (camera * PROJ + p, pl.ds(block, 1), slice(None))
                acc_ref[spot] = acc_ref[spot] + back_ref[j, p, pl.ds(camera, 1), :]
        return unused

    lax.fori_loop(0, back_ref.shape[0], gather, 0, unroll=4)
    spread = 0.375 * TSIDE
    for camera in range(2):
        first = camera * PROJ
        raw = [raw_ref[first + p] for p in range(PROJ)]
        grad = [acc_ref[first + p] for p in range(PROJ)]
        conic_a = 0.02 + 0.1 * softplus(raw[2])
        conic_c = 0.02 + 0.1 * softplus(raw[4])
        root = 0.9 * jnp.sqrt(conic_a * conic_c)
        turn = jnp.tanh(raw[3])
        from_b = 0.5 * grad[3] * root * turn
        tan_x, tan_y = jnp.tanh(raw[0]), jnp.tanh(raw[1])
        result = [
            grad[0] * spread * (1.0 - tan_x * tan_x),
            grad[1] * spread * (1.0 - tan_y * tan_y),
            (grad[2] + from_b / conic_a) * 0.1 * sigmoid(raw[2]),
            grad[3] * root * (1.0 - turn * turn),
            (grad[4] + from_b / conic_c) * 0.1 * sigmoid(raw[4]),
            grad[5] * (1.0 - sigmoid(raw[5] - 6.0)),
        ]
        for p in range(6, PROJ):
            shade = sigmoid(raw[p])
            result.append(grad[p] * shade * (1.0 - shade))
        for p in range(PROJ):
            out_ref[first + p] = result[p]


def pack_kernel(place_ref, first_ref, second_ref, *out_refs):
    for ahead, out_ref in enumerate(out_refs):
        quarter = lax.rem(place_ref[0] + ahead, 4)
        for field in range(QUARTER):
            at = jnp.minimum(quarter * QUARTER + field, FIELDS - 1)
            out_ref[0, field] = first_ref[at]
            out_ref[1, field] = second_ref[at]


def step_of(first, second, old, grad):
    new_first = BETA_FIRST * first + (1.0 - BETA_FIRST) * grad
    new_second = BETA_SECOND * second + (1.0 - BETA_SECOND) * grad * grad
    return new_first, new_second, old - RATE * new_first / (jnp.sqrt(new_second) + EPSILON)


def add_up(grads, proj_ref, source, low_ref, high_ref, blocks, fields):
    for row in range(2 * PROJ):
        value = low_ref[row, blocks, :] if row < PROJ else high_ref[row - PROJ, blocks, :]
        for at, field in enumerate(fields):
            term = proj_ref[row % PROJ, 2 * source + row // PROJ, field] * value
            grads[at] = term if grads[at] is None else grads[at] + term


def quarter_fields(place_ref, low):
    return [jnp.minimum(place_ref[0] * QUARTER + low + at, FIELDS - 1) for at in range(WIDTH)]


def near_kernel(place_ref, proj_ref, own_ref, before_low, before_high, after_low, after_high, grad_ref):
    for low in range(0, QUARTER, WIDTH):
        grads = [None] * WIDTH
        fields = quarter_fields(place_ref, low)
        own = (own_ref.at[pl.ds(0, PROJ)], own_ref.at[pl.ds(PROJ, PROJ)])
        for source, halves in enumerate((own, (before_low, before_high), (after_low, after_high))):
            add_up(grads, proj_ref, source, *halves, slice(None), fields)
        for at in range(WIDTH):
            grad_ref[low + at] = grads[at]


def quarter_kernel(
    place_ref,
    block_ref,
    live_ref,
    proj_ref,
    near_ref,
    far_low,
    far_high,
    params_ref,
    moment_0,
    moment_1,
    moment_2,
    moment_3,
    new_ref,
    parents_ref,
    grad_ref,
    held_ref,
    sem,
):
    share = moment_0.shape[2]
    base = place_ref[0] * QUARTER
    start = jnp.minimum(base, FIELDS - QUARTER)
    copy = pltpu.make_async_copy(params_ref.at[pl.ds(start, QUARTER)], held_ref, sem)
    copy.start()
    for low in range(0, QUARTER, WIDTH):
        grads = [near_ref[low + at] for at in range(WIDTH)]
        add_up(grads, proj_ref, 3, far_low, far_high, slice(None), quarter_fields(place_ref, low))
        for at in range(WIDTH):
            grad_ref[low + at] = grads[at]
    copy.wait()
    for ahead, moment_ref in enumerate((moment_0, moment_1, moment_2, moment_3)):
        blocks = pl.ds(pl.multiple_of(lax.rem(place_ref[0] + (4 - ahead), 4) * share, share), share)
        for field in range(QUARTER):
            old = held_ref[jnp.minimum(base - start + field, QUARTER - 1), blocks, :]
            new = step_of(moment_ref[0, field], moment_ref[1, field], old, grad_ref[field, blocks, :])[2]
            new_ref[field, blocks, :] = new

    def place(j, unused):
        block = block_ref[0, j]
        live = live_ref[0, j] == 1
        for field in range(QUARTER):
            parents_ref[j, field] = jnp.where(live, new_ref[field, pl.ds(block, 1), :], jnp.nan)
        return unused

    lax.fori_loop(0, parents_ref.shape[0], place, 0, unroll=8)


def moments_kernel(
    place_ref,
    proj_ref,
    own_ref,
    before_low,
    before_high,
    after_low,
    after_high,
    far_low,
    far_high,
    first_ref,
    second_ref,
    new_first_ref,
    new_second_ref,
):
    share = first_ref.shape[1]
    blocks = pl.ds(pl.multiple_of(place_ref[0] * share, share), share)
    own = (own_ref.at[pl.ds(0, PROJ)], own_ref.at[pl.ds(PROJ, PROJ)])
    sources = (own, (before_low, before_high), (after_low, after_high), (far_low, far_high))
    width = 12
    for low in range(0, FIELDS, width):
        fields = range(low, min(low + width, FIELDS))
        grads = [None] * len(fields)
        for source, halves in enumerate(sources):
            add_up(grads, proj_ref, source, *halves, blocks, fields)
        for at, field in enumerate(fields):
            first, second, unused = step_of(first_ref[field], second_ref[field], 0.0, grads[at])
            new_first_ref[field] = first
            new_second_ref[field] = second


def assemble_kernel(place_ref, own_ref, before_ref, after_ref, far_ref, out_ref):
    for field in range(QUARTER - 1, -1, -1):
        for ahead, ref in ((0, own_ref), (3, before_ref), (1, after_ref), (2, far_ref)):
            quarter = lax.rem(place_ref[0] + ahead, 4)
            out_ref[jnp.minimum(quarter * QUARTER + field, FIELDS - 1)] = ref[field]


def fill_children(ref, quarter, out_ref):
    first = quarter == 0

    def one(j, unused):
        sign = jnp.where(lax.broadcasted_iota(jnp.int32, (2, LANES), 0) == 0, 0.5, -0.5)
        rows = [jnp.broadcast_to(ref[j, field], (2, LANES)) for field in range(QUARTER)]
        for field in range(QUARTER):
            row = rows[field]
            if field < 3:
                row = row + jnp.where(first, sign * jnp.exp(rows[field + 3] - 1.0), 0.0)
            elif field < 6:
                row = row - jnp.where(first, SHRINK, 0.0)
            out_ref[j, field] = jnp.where(row != row, 0.0, row)
        return unused

    lax.fori_loop(0, out_ref.shape[0], one, 0, unroll=8)


def children_of(parts, base):
    batch = parts[0][0].shape[0] // (1 if parts[0][3] is None else 2)
    owners = 2 * batch

    def kernel(place_ref, *refs):
        out_ref = refs[-1]
        step = pl.program_id(0)
        for at, (unused, half, ahead, part) in enumerate(parts):

            @pl.when(step == at)
            def _():
                fill_children(refs[at], lax.rem(place_ref[0] + ahead, 4), out_ref)

    def pick(step, column):
        value = parts[0][column]
        for at in range(1, len(parts)):
            value = jnp.where(step == at, parts[at][column], value)
        return value

    def out_index(step, place_ref):
        return (pick(step, 1), lax.rem(place_ref[0] + pick(step, 2), 4), 0, 0)

    def in_spec(part):
        index = 0 if part is None else part
        return pl.BlockSpec((batch, QUARTER, 1, LANES), lambda step, place_ref: (index, 0, 0, 0))

    def call_on(place, *extra):
        return pl.pallas_call(
            kernel,
            out_shape=shape(owners, FIELDS, 2, LANES),
            grid_spec=pltpu.PrefetchScalarGridSpec(
                num_scalar_prefetch=1,
                grid=(len(parts),),
                in_specs=[in_spec(part) for unused, half, ahead, part in parts]
                + [pl.BlockSpec(memory_space=pl.ANY) for unused in extra],
                out_specs=pl.BlockSpec((batch, QUARTER, 2, LANES), out_index),
            ),
            input_output_aliases={len(parts) + 1: 0} if extra else {},
            compiler_params=PARAMS,
            name="children",
        )(place, *[value for value, half, ahead, part in parts], *extra)

    return call_on(*base)


def shape(*dims):
    return jax.ShapeDtypeStruct(dims, jnp.float32)


def shift_by(values, distance):
    size = lax.axis_size("cam")
    return lax.ppermute(values, "cam", [(i, (i + distance) % size) for i in range(size)])


def ring_halves(values, half):
    before_low = shift_by(values[:half], 1)
    after_high = shift_by(values[half:], 3)
    before_high = shift_by(values[half:], 1)
    after_low = shift_by(values[:half], 3)
    far = (shift_by(before_low, 1), shift_by(after_high, 3))
    return (values, before_low, before_high, after_low, after_high), far


def call(kernel, inputs, outputs, scratch=(), name=None):
    spaces = {"s": SMEM, "v": VMEM, "h": HBM}
    where = [spaces[kind] for kind, unused in inputs]
    several = isinstance(outputs, tuple)
    return pl.pallas_call(
        kernel,
        out_shape=outputs,
        in_specs=where,
        out_specs=tuple(VMEM for unused in outputs) if several else VMEM,
        scratch_shapes=list(scratch),
        compiler_params=PARAMS,
        name=name,
    )(*[value for unused, value in inputs])


def body(
    params,
    moment_first,
    moment_second,
    cam_proj,
    send_block,
    tile_slot,
    tile_count,
    targets,
    split_block,
    split_live,
):
    owned = params.shape[0]
    owners = split_block.shape[1]
    groups = lax.axis_size("cam")
    share = owned // groups
    place = lax.axis_index("cam").astype(jnp.int32).reshape(1)
    by_field = params.transpose(1, 0, 2)
    proj = cam_proj.transpose(1, 0, 2)
    send = send_block.reshape(2, owners)
    wire = shape(owners, PROJ, 2, LANES)
    rows = shape(2 * PROJ, owned, LANES)
    plane = pltpu.VMEM((2 * PROJ, owned, LANES), jnp.float32)

    def s(value):
        return ("s", value)

    def v(value):
        return ("v", value)

    outgoing, raw = pl.pallas_call(
        project_kernel,
        out_shape=(wire, rows),
        in_specs=[HBM, HBM, HBM],
        out_specs=(VMEM, VMEM),
        scratch_shapes=[
            pltpu.VMEM((FIELDS, owned, LANES), jnp.float32),
            pltpu.VMEM((2 * PROJ, owned, LANES), jnp.float32),
            pltpu.SMEM((PROJ, 2, FIELDS), jnp.float32),
            pltpu.SMEM((2, owners), jnp.int32),
            pltpu.SemaphoreType.DMA((6,)),
        ],
        compiler_params=pltpu.CompilerParams(vmem_limit_bytes=62 * 1024 * 1024),
        name="project",
    )(proj, send, by_field)
    received = lax.all_to_all(outgoing, "dev", split_axis=0, concat_axis=0, tiled=True)

    projs = jnp.concatenate([proj, shift_by(proj, 1), shift_by(proj, 3), shift_by(proj, 2)], axis=1)
    plan = jnp.concatenate([tile_slot.reshape(2, 2 * KMAX), tile_count], axis=1)
    target = jnp.broadcast_to(targets.reshape(12, PIX, 1), (12, PIX, LANES))
    received, target, plan, projs = lax.optimization_barrier((received, target, plan, projs))

    returning, pictures = call(
        render_kernel, [s(plan), v(received), v(target)], (wire, shape(PIX, LANES)), RENDER_SCRATCH, "render"
    )
    returned = lax.all_to_all(returning, "dev", split_axis=0, concat_axis=0, tiled=True)

    first = moment_first.reshape(share, FIELDS, LANES).transpose(1, 0, 2)
    second = moment_second.reshape(share, FIELDS, LANES).transpose(1, 0, 2)
    first, second, returning = lax.optimization_barrier((first, second, returning))
    packed = call(
        pack_kernel, [s(place), v(first), v(second)], tuple(shape(2, QUARTER, share, LANES) for unused in range(4)), (), "pack"
    )
    moments = [packed[0]] + [shift_by(packed[ahead], ahead) for ahead in range(1, 4)]
    images = pictures[:, :12].T.reshape(targets.shape)
    returned, moments, images = lax.optimization_barrier((returned, moments, images))
    pulls = call(collect_kernel, [s(send), v(returned), v(raw)], rows, [plane], "collect")
    near, far = ring_halves(pulls, PROJ)
    near, far = [v(value) for value in near], [v(value) for value in far]
    grads = call(near_kernel, [s(place), s(projs)] + near, shape(QUARTER, owned, LANES), (), "near")
    fresh, parents = call(
        quarter_kernel,
        [s(place), s(split_block), s(split_live), s(projs), v(grads)]
        + far
        + [("h", by_field)]
        + [v(value) for value in moments],
        (shape(QUARTER, owned, LANES), shape(owners, QUARTER, 1, LANES)),
        [
            pltpu.VMEM((QUARTER, owned, LANES), jnp.float32),
            pltpu.VMEM((QUARTER, owned, LANES), jnp.float32),
            pltpu.SemaphoreType.DMA(()),
        ],
        "quarter",
    )
    parents = lax.all_to_all(parents, "dev", split_axis=0, concat_axis=0, tiled=True)
    own = shape(FIELDS, share, LANES)
    new_first, new_second = call(
        moments_kernel, [s(place), s(projs)] + near + far + [v(first), v(second)], (own, own), (), "moments"
    )
    before, after = shift_by(fresh, 1), shift_by(fresh, 3)
    fresh = (fresh, before, after, shift_by(fresh, 2))
    parents, new_first, new_second, fresh = lax.optimization_barrier((parents, new_first, new_second, fresh))
    fresh = [v(value) for value in fresh]
    new_params = call(assemble_kernel, [s(place)] + fresh, shape(FIELDS, owned, LANES), (), "assemble")
    near, far = ring_halves(parents, owners // 2)
    own, before_low, before_high, after_low, after_high = near
    before_high, new_params = lax.optimization_barrier((before_high, new_params))
    children = children_of([(own, 0, 0, 0), (own, 1, 0, 1)], (place,))
    children = children_of(
        [(before_low, 0, 3, None), (before_high, 1, 3, None), (after_low, 0, 1, None), (after_high, 1, 1, None)],
        (place, children),
    )
    children = children_of([(far[1], 1, 2, None)], (place, children))
    children = children_of([(far[0], 0, 2, None)], (place, children))

    def back(values):
        return values.transpose(1, 0, 2).reshape(moment_first.shape)

    return (
        images,
        new_params.transpose(1, 0, 2),
        back(new_first),
        back(new_second),
        children.transpose(0, 2, 1, 3),
    )


def solution(mesh):
    placed = (
        P("dev", None, None),
        P("dev", "cam", None, None, None),
        P("dev", "cam", None, None, None),
        P("cam", None, None),
        P("cam", "dev", None, None),
        P("cam", "dev", None),
        P("cam", "dev"),
        P("cam", "dev", None, None),
        P("dev", None),
        P("dev", None),
    )
    return jax.shard_map(
        body,
        mesh=mesh,
        in_specs=placed,
        out_specs=(
            P("cam", "dev", None, None),
            P("dev", None, None),
            P("dev", "cam", None, None, None),
            P("dev", "cam", None, None, None),
            P("dev", None, None, None),
        ),
        check_vma=False,
    )
```

```python
import math

import jax
import jax.numpy as jnp
from jax import lax
from jax.experimental import pallas as pl
from jax.experimental.pallas import tpu as pltpu
from jax.sharding import PartitionSpec as P

TSIDE = 16
PIX = TSIDE * TSIDE
LANES = 128
PROJ = 9
KMAX = 8
FIELDS = 59
QUARTER = 15
WIDTH = 5

LOSS_WEIGHT = 256.0
RATE = 0.01
BETA_FIRST = 0.9
BETA_SECOND = 0.999
EPSILON = 1e-08
SHRINK = math.log(1.6)
LOG2E = math.log2(math.e)

VMEM = pl.BlockSpec(memory_space=pltpu.VMEM)
SMEM = pl.BlockSpec(memory_space=pltpu.SMEM)
HBM = pl.BlockSpec(memory_space=pltpu.HBM)
PARAMS = pltpu.CompilerParams(vmem_limit_bytes=40 * 1024 * 1024)


def softplus(values):
    return jnp.maximum(values, 0.0) + jnp.log1p(jnp.exp(-jnp.abs(values)))


def sigmoid(values):
    return 1.0 / (1.0 + jnp.exp(-values))


def project_kernel(proj_in, send_in, params_ref, out_ref, raw_ref, held_ref, feat_ref, proj_ref, send_ref, sems):
    centre, spread = 0.5 * TSIDE, 0.375 * TSIDE
    copies = []
    for part, low in enumerate(range(0, FIELDS, QUARTER)):
        rows = pl.ds(low, min(QUARTER, FIELDS - low))
        copies.append(pltpu.make_async_copy(params_ref.at[rows], held_ref.at[rows], sems.at[part]))
        copies[-1].start()
    lists = pltpu.make_async_copy(send_in, send_ref, sems.at[4])
    weights = pltpu.make_async_copy(proj_in, proj_ref, sems.at[5])
    weights.start()
    lists.start()
    weights.wait()
    lists.wait()
    for part, copy in enumerate(copies):
        copy.wait()
        low = part * QUARTER
        for camera in range(2):
            raw = [None] * PROJ if part == 0 else [raw_ref[camera * PROJ + p] for p in range(PROJ)]
            for field in range(low, min(low + QUARTER, FIELDS)):
                row = held_ref[field]
                for p in range(PROJ):
                    term = proj_ref[p, camera, field] * row
                    raw[p] = term if field == 0 else raw[p] + term
            for p in range(PROJ):
                raw_ref[camera * PROJ + p] = raw[p]
    for camera in range(2):
        first = camera * PROJ
        raw = [raw_ref[first + p] for p in range(PROJ)]
        conic_a = 0.02 + 0.1 * softplus(raw[2])
        conic_c = 0.02 + 0.1 * softplus(raw[4])
        feat_ref[first + 0] = centre + spread * jnp.tanh(raw[0])
        feat_ref[first + 1] = centre + spread * jnp.tanh(raw[1])
        feat_ref[first + 2] = conic_a
        feat_ref[first + 3] = 0.9 * jnp.sqrt(conic_a * conic_c) * jnp.tanh(raw[3])
        feat_ref[first + 4] = conic_c
        feat_ref[first + 5] = 0.99 * sigmoid(raw[5] - 6.0)
        for p in range(6, PROJ):
            feat_ref[first + p] = sigmoid(raw[p])

    def place(j, unused):
        for camera in range(2):
            block = send_ref[camera, j]
            for p in range(PROJ):
                out_ref[j, p, pl.ds(camera, 1), :] = feat_ref[camera * PROJ + p, pl.ds(block, 1), :]
        return unused

    lax.fori_loop(0, out_ref.shape[0], place, 0, unroll=8)


SPLITS = 2


def split_parts(values):
    parts = []
    for at in range(SPLITS):
        part = values.astype(jnp.bfloat16)
        parts.append(part)
        if at < SPLITS - 1:
            values = values - part.astype(jnp.float32)
    return parts


def render_kernel(
    plan_ref,
    recv_ref,
    target_ref,
    back_ref,
    image_ref,
    alpha_ref,
    weight_ref,
    shade_ref,
    part_ref,
    before_ref,
    behind_ref,
    acc_ref,
    carry_ref,
):
    lane = lax.broadcasted_iota(jnp.int32, (PIX, LANES), 1)
    column = lax.broadcasted_iota(jnp.int32, (TSIDE, LANES), 0).astype(jnp.float32) + 0.5
    row = lax.broadcasted_iota(jnp.int32, (LANES, 2 * LANES), 0)
    col = lax.broadcasted_iota(jnp.int32, (LANES, 2 * LANES), 1)
    earlier = jnp.where((row < col) | (col >= LANES), 1.0, 0.0).astype(jnp.bfloat16)
    later = jnp.where((row > col) | (col >= LANES), 1.0, 0.0).astype(jnp.bfloat16)
    for at in range(SPLITS):
        before_ref[at * LANES : (at + 1) * LANES] = earlier
        behind_ref[at * LANES : (at + 1) * LANES] = later
    back_ref[...] = jnp.zeros(back_ref.shape, jnp.float32)
    image_ref[...] = jnp.zeros(image_ref.shape, jnp.float32)

    def tile(index, unused):
        camera = index // 2
        which = index % 2
        count = plan_ref[camera, 2 * KMAX + which]
        pairs = (count + 1) // 2

        def slot_at(k):
            return plan_ref[camera, which * KMAX + jnp.minimum(k, count - 1)]

        def feature(slot, p):
            return recv_ref[slot, p, pl.ds(camera, 1), :]

        def put_parts(start, values):
            for at, part in enumerate(split_parts(values)):
                part_ref[start : start + values.shape[0], at * LANES : (at + 1) * LANES] = part

        carry_ref[...] = jnp.zeros(carry_ref.shape, jnp.float32)
        acc_ref[...] = jnp.zeros(acc_ref.shape, jnp.float32)

        def forward(pair, unused):
            slots = [slot_at(pair * 2 + e) for e in range(2)]
            for e in range(2):
                k = pair * 2 + e
                slot = slots[e]
                opacity = jnp.where(k < count, feature(slot, 5), 0.0)
                off_x = column - feature(slot, 0)
                mean_y = feature(slot, 1)
                half_a = (-0.5 * LOG2E) * feature(slot, 2)
                full_b = -LOG2E * feature(slot, 3)
                half_c = (-0.5 * LOG2E) * feature(slot, 4)
                square_x = half_a * off_x * off_x
                for y in range(TSIDE):
                    off_y = (y + 0.5) - mean_y
                    alpha = opacity * jnp.exp2(square_x + ((full_b * off_y) * off_x + half_c * off_y * off_y))
                    alpha_ref[k, y * TSIDE : (y + 1) * TSIDE] = alpha
                    put_parts(e * PIX + y * TSIDE, jnp.log(1.0 - alpha))
            sums = jnp.dot(part_ref[...], before_ref[...], preferred_element_type=jnp.float32)
            colours = [[feature(slots[e], 6 + c) for c in range(3)] for e in range(2)]
            for y in range(TSIDE):
                rows = slice(y * TSIDE, (y + 1) * TSIDE)
                next_rows = slice(PIX + y * TSIDE, PIX + (y + 1) * TSIDE)
                carry = carry_ref[rows]
                weights = [alpha_ref[pair * 2, rows] * jnp.exp(carry + sums[rows, :LANES])]
                carry = carry + sums[rows, LANES:]
                weights.append(alpha_ref[pair * 2 + 1, rows] * jnp.exp(carry + sums[next_rows, :LANES]))
                carry_ref[rows] = carry + sums[next_rows, LANES:]
                weight_ref[pair * 2, rows] = weights[0]
                weight_ref[pair * 2 + 1, rows] = weights[1]
                for c in range(3):
                    acc_ref[c, rows] = acc_ref[c, rows] + (colours[0][c] * weights[0] + colours[1][c] * weights[1])
            return unused

        lax.fori_loop(0, pairs, forward, 0)
        for c in range(3):
            place = index * 3 + c
            put_parts(0, acc_ref[c])
            colour = jnp.dot(part_ref[:PIX], before_ref[:, LANES:], preferred_element_type=jnp.float32)
            image_ref[...] = jnp.where(lane == place, colour, image_ref[...])
            acc_ref[c] = LOSS_WEIGHT * (colour - target_ref[place])
        carry_ref[...] = jnp.zeros(carry_ref.shape, jnp.float32)

        def backward(step, unused):
            pair = pairs - 1 - step
            slots = [slot_at(pair * 2 + e) for e in range(2)]
            colour_grads = []
            for e in range(2):
                k = pair * 2 + e
                colours = [feature(slots[e], 6 + c) for c in range(3)]
                sums_c = [None] * 3
                for y in range(TSIDE):
                    rows = slice(y * TSIDE, (y + 1) * TSIDE)
                    weights = weight_ref[k, rows]
                    cots = [acc_ref[c, rows] for c in range(3)]
                    shade = (colours[0] * cots[0] + colours[1] * cots[1] + colours[2] * cots[2]) * weights
                    shade_ref[e, rows] = shade
                    put_parts(e * PIX + y * TSIDE, shade)
                    for c in range(3):
                        term = cots[c] * weights
                        sums_c[c] = term if y == 0 else sums_c[c] + term
                colour_grads.append(sums_c)
            sums = jnp.dot(part_ref[...], behind_ref[...], preferred_element_type=jnp.float32)
            for e in (1, 0):
                k = pair * 2 + e
                slot = slots[e]
                off_x = column - feature(slot, 0)
                mean_y = feature(slot, 1)
                plain, first_y, second_y = None, None, None
                for y in range(TSIDE):
                    rows = slice(y * TSIDE, (y + 1) * TSIDE)
                    inside = slice(e * PIX + y * TSIDE, e * PIX + (y + 1) * TSIDE)
                    carry = carry_ref[rows]
                    alpha = alpha_ref[k, rows]
                    keep = 1.0 - alpha
                    inverse = pl.reciprocal(keep, approx=True)
                    inverse = inverse * (2.0 - keep * inverse)
                    pull = shade_ref[e, rows] - (carry + sums[inside, :LANES]) * (alpha * inverse)
                    carry_ref[rows] = carry + sums[inside, LANES:]
                    off_y = (y + 0.5) - mean_y
                    once = off_y * pull
                    twice = off_y * once
                    plain = pull if y == 0 else plain + pull
                    first_y = once if y == 0 else first_y + once
                    second_y = twice if y == 0 else second_y + twice

                def total(values):
                    return jnp.sum(values, axis=0, keepdims=True)

                along_x = off_x * plain
                sum_x = total(along_x)
                sum_y = total(first_y)
                conic_a, conic_b, conic_c = feature(slot, 2), feature(slot, 3), feature(slot, 4)
                grads = [
                    conic_a * sum_x + conic_b * sum_y,
                    conic_b * sum_x + conic_c * sum_y,
                    -0.5 * total(off_x * along_x),
                    -total(off_x * first_y),
                    -0.5 * total(second_y),
                    total(plain),
                ] + [total(values) for values in colour_grads[e]]
                for p in range(PROJ):
                    spot = (slot, p, pl.ds(camera, 1), slice(None))
                    back_ref[spot] = back_ref[spot] + grads[p]
            return unused

        lax.fori_loop(0, pairs, backward, 0)
        return unused

    lax.fori_loop(0, 4, tile, 0)


RENDER_SCRATCH = [
    pltpu.VMEM((8, PIX, LANES), jnp.float32),
    pltpu.VMEM((8, PIX, LANES), jnp.float32),
    pltpu.VMEM((2, PIX, LANES), jnp.float32),
    pltpu.VMEM((2 * PIX, SPLITS * LANES), jnp.bfloat16),
    pltpu.VMEM((SPLITS * LANES, 2 * LANES), jnp.bfloat16),
    pltpu.VMEM((SPLITS * LANES, 2 * LANES), jnp.bfloat16),
    pltpu.VMEM((3, PIX, LANES), jnp.float32),
    pltpu.VMEM((PIX, LANES), jnp.float32),
]


def collect_kernel(send_ref, back_ref, raw_ref, out_ref, acc_ref):
    acc_ref[...] = jnp.zeros(acc_ref.shape, jnp.float32)

    def gather(j, unused):
        for camera in range(2):
            block = send_ref[camera, j]
            for p in range(PROJ):
                spot = (camera * PROJ + p, pl.ds(block, 1), slice(None))
                acc_ref[spot] = acc_ref[spot] + back_ref[j, p, pl.ds(camera, 1), :]
        return unused

    lax.fori_loop(0, back_ref.shape[0], gather, 0, unroll=4)
    spread = 0.375 * TSIDE
    for camera in range(2):
        first = camera * PROJ
        raw = [raw_ref[first + p] for p in range(PROJ)]
        grad = [acc_ref[first + p] for p in range(PROJ)]
        conic_a = 0.02 + 0.1 * softplus(raw[2])
        conic_c = 0.02 + 0.1 * softplus(raw[4])
        root = 0.9 * jnp.sqrt(conic_a * conic_c)
        turn = jnp.tanh(raw[3])
        from_b = 0.5 * grad[3] * root * turn
        tan_x, tan_y = jnp.tanh(raw[0]), jnp.tanh(raw[1])
        result = [
            grad[0] * spread * (1.0 - tan_x * tan_x),
            grad[1] * spread * (1.0 - tan_y * tan_y),
            (grad[2] + from_b / conic_a) * 0.1 * sigmoid(raw[2]),
            grad[3] * root * (1.0 - turn * turn),
            (grad[4] + from_b / conic_c) * 0.1 * sigmoid(raw[4]),
            grad[5] * (1.0 - sigmoid(raw[5] - 6.0)),
        ]
        for p in range(6, PROJ):
            shade = sigmoid(raw[p])
            result.append(grad[p] * shade * (1.0 - shade))
        for p in range(PROJ):
            out_ref[first + p] = result[p]


def pack_kernel(place_ref, first_ref, second_ref, *out_refs):
    for ahead, out_ref in enumerate(out_refs):
        quarter = lax.rem(place_ref[0] + ahead, 4)
        for field in range(QUARTER):
            at = jnp.minimum(quarter * QUARTER + field, FIELDS - 1)
            out_ref[0, field] = first_ref[at]
            out_ref[1, field] = second_ref[at]


def step_of(first, second, old, grad):
    new_first = BETA_FIRST * first + (1.0 - BETA_FIRST) * grad
    new_second = BETA_SECOND * second + (1.0 - BETA_SECOND) * grad * grad
    return new_first, new_second, old - RATE * new_first / (jnp.sqrt(new_second) + EPSILON)


def add_up(grads, proj_ref, source, low_ref, high_ref, blocks, fields):
    for row in range(2 * PROJ):
        value = low_ref[row, blocks, :] if row < PROJ else high_ref[row - PROJ, blocks, :]
        for at, field in enumerate(fields):
            term = proj_ref[row % PROJ, 2 * source + row // PROJ, field] * value
            grads[at] = term if grads[at] is None else grads[at] + term


def quarter_fields(place_ref, low):
    return [jnp.minimum(place_ref[0] * QUARTER + low + at, FIELDS - 1) for at in range(WIDTH)]


def near_kernel(place_ref, proj_ref, own_ref, before_low, before_high, after_low, after_high, grad_ref):
    for low in range(0, QUARTER, WIDTH):
        grads = [None] * WIDTH
        fields = quarter_fields(place_ref, low)
        own = (own_ref.at[pl.ds(0, PROJ)], own_ref.at[pl.ds(PROJ, PROJ)])
        for source, halves in enumerate((own, (before_low, before_high), (after_low, after_high))):
            add_up(grads, proj_ref, source, *halves, slice(None), fields)
        for at in range(WIDTH):
            grad_ref[low + at] = grads[at]


def quarter_kernel(
    place_ref,
    block_ref,
    live_ref,
    proj_ref,
    near_ref,
    far_low,
    far_high,
    params_ref,
    moment_0,
    moment_1,
    moment_2,
    moment_3,
    new_ref,
    parents_ref,
    grad_ref,
    held_ref,
    sem,
):
    share = moment_0.shape[2]
    base = place_ref[0] * QUARTER
    start = jnp.minimum(base, FIELDS - QUARTER)
    copy = pltpu.make_async_copy(params_ref.at[pl.ds(start, QUARTER)], held_ref, sem)
    copy.start()
    for low in range(0, QUARTER, WIDTH):
        grads = [near_ref[low + at] for at in range(WIDTH)]
        add_up(grads, proj_ref, 3, far_low, far_high, slice(None), quarter_fields(place_ref, low))
        for at in range(WIDTH):
            grad_ref[low + at] = grads[at]
    copy.wait()
    for ahead, moment_ref in enumerate((moment_0, moment_1, moment_2, moment_3)):
        blocks = pl.ds(pl.multiple_of(lax.rem(place_ref[0] + (4 - ahead), 4) * share, share), share)
        for field in range(QUARTER):
            old = held_ref[jnp.minimum(base - start + field, QUARTER - 1), blocks, :]
            new = step_of(moment_ref[0, field], moment_ref[1, field], old, grad_ref[field, blocks, :])[2]
            new_ref[field, blocks, :] = new

    def place(j, unused):
        block = block_ref[0, j]
        live = live_ref[0, j] == 1
        for field in range(QUARTER):
            parents_ref[j, field] = jnp.where(live, new_ref[field, pl.ds(block, 1), :], jnp.nan)
        return unused

    lax.fori_loop(0, parents_ref.shape[0], place, 0, unroll=8)


def moments_kernel(
    place_ref,
    proj_ref,
    own_ref,
    before_low,
    before_high,
    after_low,
    after_high,
    far_low,
    far_high,
    first_ref,
    second_ref,
    new_first_ref,
    new_second_ref,
):
    share = first_ref.shape[1]
    blocks = pl.ds(pl.multiple_of(place_ref[0] * share, share), share)
    own = (own_ref.at[pl.ds(0, PROJ)], own_ref.at[pl.ds(PROJ, PROJ)])
    sources = (own, (before_low, before_high), (after_low, after_high), (far_low, far_high))
    width = 12
    for low in range(0, FIELDS, width):
        fields = range(low, min(low + width, FIELDS))
        grads = [None] * len(fields)
        for source, halves in enumerate(sources):
            add_up(grads, proj_ref, source, *halves, blocks, fields)
        for at, field in enumerate(fields):
            first, second, unused = step_of(first_ref[field], second_ref[field], 0.0, grads[at])
            new_first_ref[field] = first
            new_second_ref[field] = second


def assemble_kernel(place_ref, own_ref, before_ref, after_ref, far_ref, out_ref):
    for field in range(QUARTER - 1, -1, -1):
        for ahead, ref in ((0, own_ref), (3, before_ref), (1, after_ref), (2, far_ref)):
            quarter = lax.rem(place_ref[0] + ahead, 4)
            out_ref[jnp.minimum(quarter * QUARTER + field, FIELDS - 1)] = ref[field]


def fill_children(ref, quarter, out_ref):
    first = quarter == 0

    def one(j, unused):
        sign = jnp.where(lax.broadcasted_iota(jnp.int32, (2, LANES), 0) == 0, 0.5, -0.5)
        rows = [jnp.broadcast_to(ref[j, field], (2, LANES)) for field in range(QUARTER)]
        for field in range(QUARTER):
            row = rows[field]
            if field < 3:
                row = row + jnp.where(first, sign * jnp.exp(rows[field + 3] - 1.0), 0.0)
            elif field < 6:
                row = row - jnp.where(first, SHRINK, 0.0)
            out_ref[j, field] = jnp.where(row != row, 0.0, row)
        return unused

    lax.fori_loop(0, out_ref.shape[0], one, 0, unroll=8)


def children_of(parts, base):
    batch = parts[0][0].shape[0] // (1 if parts[0][3] is None else 2)
    owners = 2 * batch

    def kernel(place_ref, *refs):
        out_ref = refs[-1]
        step = pl.program_id(0)
        for at, (unused, half, ahead, part) in enumerate(parts):

            @pl.when(step == at)
            def _():
                fill_children(refs[at], lax.rem(place_ref[0] + ahead, 4), out_ref)

    def pick(step, column):
        value = parts[0][column]
        for at in range(1, len(parts)):
            value = jnp.where(step == at, parts[at][column], value)
        return value

    def out_index(step, place_ref):
        return (pick(step, 1), lax.rem(place_ref[0] + pick(step, 2), 4), 0, 0)

    def in_spec(part):
        index = 0 if part is None else part
        return pl.BlockSpec((batch, QUARTER, 1, LANES), lambda step, place_ref: (index, 0, 0, 0))

    def call_on(place, *extra):
        return pl.pallas_call(
            kernel,
            out_shape=shape(owners, FIELDS, 2, LANES),
            grid_spec=pltpu.PrefetchScalarGridSpec(
                num_scalar_prefetch=1,
                grid=(len(parts),),
                in_specs=[in_spec(part) for unused, half, ahead, part in parts]
                + [pl.BlockSpec(memory_space=pl.ANY) for unused in extra],
                out_specs=pl.BlockSpec((batch, QUARTER, 2, LANES), out_index),
            ),
            input_output_aliases={len(parts) + 1: 0} if extra else {},
            compiler_params=PARAMS,
            name="children",
        )(place, *[value for value, half, ahead, part in parts], *extra)

    return call_on(*base)


def shape(*dims):
    return jax.ShapeDtypeStruct(dims, jnp.float32)


def shift_by(values, distance):
    size = lax.axis_size("cam")
    return lax.ppermute(values, "cam", [(i, (i + distance) % size) for i in range(size)])


def ring_halves(values, half):
    before_low = shift_by(values[:half], 1)
    after_high = shift_by(values[half:], 3)
    before_high = shift_by(values[half:], 1)
    after_low = shift_by(values[:half], 3)
    far = (shift_by(before_low, 1), shift_by(after_high, 3))
    return (values, before_low, before_high, after_low, after_high), far


def call(kernel, inputs, outputs, scratch=(), name=None):
    spaces = {"s": SMEM, "v": VMEM, "h": HBM}
    where = [spaces[kind] for kind, unused in inputs]
    several = isinstance(outputs, tuple)
    return pl.pallas_call(
        kernel,
        out_shape=outputs,
        in_specs=where,
        out_specs=tuple(VMEM for unused in outputs) if several else VMEM,
        scratch_shapes=list(scratch),
        compiler_params=PARAMS,
        name=name,
    )(*[value for unused, value in inputs])


def body(
    params,
    moment_first,
    moment_second,
    cam_proj,
    send_block,
    tile_slot,
    tile_count,
    targets,
    split_block,
    split_live,
):
    owned = params.shape[0]
    owners = split_block.shape[1]
    groups = lax.axis_size("cam")
    share = owned // groups
    place = lax.axis_index("cam").astype(jnp.int32).reshape(1)
    by_field = params.transpose(1, 0, 2)
    proj = cam_proj.transpose(1, 0, 2)
    send = send_block.reshape(2, owners)
    wire = shape(owners, PROJ, 2, LANES)
    rows = shape(2 * PROJ, owned, LANES)
    plane = pltpu.VMEM((2 * PROJ, owned, LANES), jnp.float32)

    def s(value):
        return ("s", value)

    def v(value):
        return ("v", value)

    outgoing, raw = pl.pallas_call(
        project_kernel,
        out_shape=(wire, rows),
        in_specs=[HBM, HBM, HBM],
        out_specs=(VMEM, VMEM),
        scratch_shapes=[
            pltpu.VMEM((FIELDS, owned, LANES), jnp.float32),
            pltpu.VMEM((2 * PROJ, owned, LANES), jnp.float32),
            pltpu.SMEM((PROJ, 2, FIELDS), jnp.float32),
            pltpu.SMEM((2, owners), jnp.int32),
            pltpu.SemaphoreType.DMA((6,)),
        ],
        compiler_params=pltpu.CompilerParams(vmem_limit_bytes=62 * 1024 * 1024),
        name="project",
    )(proj, send, by_field)
    received = lax.all_to_all(outgoing, "dev", split_axis=0, concat_axis=0, tiled=True)

    plan = jnp.concatenate([tile_slot.reshape(2, 2 * KMAX), tile_count], axis=1)
    target = jnp.broadcast_to(targets.reshape(12, PIX, 1), (12, PIX, LANES))
    others = [shift_by(proj, distance) for distance in (1, 3, 2)]
    others, target = lax.optimization_barrier((others, target))
    projs = jnp.concatenate([proj] + others, axis=1)
    received, target, plan, projs = lax.optimization_barrier((received, target, plan, projs))

    returning, pictures = call(
        render_kernel, [s(plan), v(received), v(target)], (wire, shape(PIX, LANES)), RENDER_SCRATCH, "render"
    )
    returned = lax.all_to_all(returning, "dev", split_axis=0, concat_axis=0, tiled=True)

    first = moment_first.reshape(share, FIELDS, LANES).transpose(1, 0, 2)
    second = moment_second.reshape(share, FIELDS, LANES).transpose(1, 0, 2)
    first, second, returning = lax.optimization_barrier((first, second, returning))
    packed = call(
        pack_kernel, [s(place), v(first), v(second)], tuple(shape(2, QUARTER, share, LANES) for unused in range(4)), (), "pack"
    )
    moments = [packed[0]] + [shift_by(packed[ahead], ahead) for ahead in range(1, 4)]
    images = pictures[:, :12].T.reshape(targets.shape)
    returned, moments, images = lax.optimization_barrier((returned, moments, images))
    pulls = call(collect_kernel, [s(send), v(returned), v(raw)], rows, [plane], "collect")
    near, far = ring_halves(pulls, PROJ)
    near, far = [v(value) for value in near], [v(value) for value in far]
    grads = call(near_kernel, [s(place), s(projs)] + near, shape(QUARTER, owned, LANES), (), "near")
    fresh, parents = call(
        quarter_kernel,
        [s(place), s(split_block), s(split_live), s(projs), v(grads)]
        + far
        + [("h", by_field)]
        + [v(value) for value in moments],
        (shape(QUARTER, owned, LANES), shape(owners, QUARTER, 1, LANES)),
        [
            pltpu.VMEM((QUARTER, owned, LANES), jnp.float32),
            pltpu.VMEM((QUARTER, owned, LANES), jnp.float32),
            pltpu.SemaphoreType.DMA(()),
        ],
        "quarter",
    )
    parents = lax.all_to_all(parents, "dev", split_axis=0, concat_axis=0, tiled=True)
    own = shape(FIELDS, share, LANES)
    new_first, new_second = call(
        moments_kernel, [s(place), s(projs)] + near + far + [v(first), v(second)], (own, own), (), "moments"
    )
    before, after = shift_by(fresh, 1), shift_by(fresh, 3)
    fresh = (fresh, before, after, shift_by(fresh, 2))
    parents, new_first, new_second, fresh = lax.optimization_barrier((parents, new_first, new_second, fresh))
    fresh = [v(value) for value in fresh]
    new_params = call(assemble_kernel, [s(place)] + fresh, shape(FIELDS, owned, LANES), (), "assemble")
    near, far = ring_halves(parents, owners // 2)
    own, before_low, before_high, after_low, after_high = near
    before_high, new_params = lax.optimization_barrier((before_high, new_params))
    children = children_of([(own, 0, 0, 0), (own, 1, 0, 1)], (place,))
    children = children_of(
        [(before_low, 0, 3, None), (before_high, 1, 3, None), (after_low, 0, 1, None), (after_high, 1, 1, None)],
        (place, children),
    )
    children = children_of([(far[1], 1, 2, None)], (place, children))
    children = children_of([(far[0], 0, 2, None)], (place, children))

    def back(values):
        return values.transpose(1, 0, 2).reshape(moment_first.shape)

    return (
        images,
        new_params.transpose(1, 0, 2),
        back(new_first),
        back(new_second),
        children.transpose(0, 2, 1, 3),
    )


def solution(mesh):
    placed = (
        P("dev", None, None),
        P("dev", "cam", None, None, None),
        P("dev", "cam", None, None, None),
        P("cam", None, None),
        P("cam", "dev", None, None),
        P("cam", "dev", None),
        P("cam", "dev"),
        P("cam", "dev", None, None),
        P("dev", None),
        P("dev", None),
    )
    return jax.shard_map(
        body,
        mesh=mesh,
        in_specs=placed,
        out_specs=(
            P("cam", "dev", None, None),
            P("dev", None, None),
            P("dev", "cam", None, None, None),
            P("dev", "cam", None, None, None),
            P("dev", None, None, None),
        ),
        check_vma=False,
    )
```
